256 devices in a mesh: grp: 8 (over x, y_hi), hid: 32 (over z, y_lo, core).
Axes of the slice: x: 4, y: 4 (y_hi: 2, y_lo: 2; y = y_hi * 2 + y_lo), z: 8, core: 2. Of those that a mesh axis runs over, the one named last changes fastest.
Arguments:
- train_acts: bfloat16 [2048, 64, 4096], P('grp', None, 'hid'), may hold values from -6 to 6
- train_cots: bfloat16 [2048, 64, 4096], P('grp', None, 'hid'), may hold values from -6 to 6
- train_len: int32 [2048], P('grp'), may hold values from 16 to 64
- test_grads: bfloat16 [40960, 4096], P(('hid', 'grp')), may hold values from -0.01171875 to 0.01171875
- proj_in: bfloat16 [64, 4096], P(None, 'hid'), may hold values from -0.09375 to 0.09375
- proj_out: bfloat16 [64, 4096], P(None, 'hid'), may hold values from -0.09375 to 0.09375
Outputs:
- scores: float32 [2048, 40960], P('grp', 'hid')
The draws below stay inside these ranges and needn't reach their ends.
All inputs are finite; a program needn't handle non-finite values.
Results may differ from the reference program's by a relative error of at most 0.0029.
Values may be sent and summed in bfloat16 or wider, within the bound.
No kernel may reach another device: no remote copies, remote signals or barrier semaphores. Data moves between devices by JAX's collectives and lax.ppermute only.
A program may use at most 128 MiB of HBM per device.

```python
import jax
import jax.numpy as jnp
from jax import lax

D = 4096
K = 64
SEQ = 64
KK = 4096
TRAIN = 2048
TEST = 40960


def with_ends(array, stream_key, smallest, largest):
    spot = [jax.random.randint(jax.random.fold_in(stream_key, axis), (), 0, length) for axis, length in enumerate(array.shape)]
    longest = array.shape.index(max(array.shape))
    next_to = spot[:longest] + [(spot[longest] + 1) % array.shape[longest]] + spot[longest + 1:]
    return array.at[tuple(spot)].set(smallest).at[tuple(next_to)].set(largest)


def spiked(result, rng, source, target, shards_of, factor):
    def block_of(axis_at):
        return (jnp.arange(result.shape[axis_at]) // (result.shape[axis_at] // shards_of)).reshape((-1,) + (1,) * (result.ndim - 1 - axis_at))

    near = jax.random.permutation(rng, shards_of)[block_of(target)]
    far = (block_of(target) + shards_of // 2) % shards_of
    return jnp.where((block_of(source) == near) | (block_of(source) == far), factor * result, result)


def block_levels(own_key, dims, split, low, largest):
    def one(dim, parts):
        steps = jax.random.uniform(jax.random.fold_in(jax.random.fold_in(own_key, 6), dim), (parts,), jnp.float32, low / len(split), largest / len(split))
        return jnp.repeat(jnp.exp(steps), dims[dim] // parts).reshape((-1,) + (1,) * (len(dims) - dim - 1))

    loudness = one(*split[0])
    for cut in split[1:]:
        loudness = loudness * one(*cut)
    return loudness


def gaussian(rng, shape, spread, most, shards=(), kind=jnp.bfloat16):
    array = jax.random.normal(rng, shape, jnp.float32) * spread
    if len(shards) > 0:
        array = block_levels(rng, shape, shards, -0.22, 0.18) * array
    return jnp.clip(array, min=-most, max=most).astype(kind)


def noise_with(rng, dims, width, bound, cuts, heavy, kind=jnp.bfloat16):
    result = width * jax.random.normal(rng, dims, jnp.float32)
    if cuts:
        result = result * block_levels(rng, dims, cuts, -0.22, 0.18)
    return jnp.clip(spiked(result, jax.random.fold_in(rng, 3), *heavy), -bound, bound).astype(kind)


def setup_inputs(seed: int = 0) -> dict:
    splits = jax.random.split(jax.random.key(seed), 7)
    return {
        "train_acts": noise_with(splits[0], (TRAIN, SEQ, D), 1.0, 6.0, ((0, 8), (2, 32)), (2, 0, 32, 2.75)),
        "train_cots": gaussian(splits[1], (TRAIN, SEQ, D), 1.0, 6.0, ((0, 8), (2, 32))),
        "train_len": with_ends(jax.random.randint(splits[2], (TRAIN,), SEQ // 4, SEQ + 1), jax.random.fold_in(splits[2], 1), SEQ // 4, SEQ).astype(jnp.int32),
        "test_grads": gaussian(splits[3], (TEST, KK), (K * K * SEQ) ** -0.5, 0.01171875, ((0, 256),)),
        "proj_in": gaussian(splits[4], (K, D), D ** -0.5, 0.09375, ((1, 32),)),
        "proj_out": gaussian(splits[5], (K, D), D ** -0.5, 0.09375, ((1, 32),)),
    }


def project_side(values, weight, token_mask):
    flat = values.reshape(-1, values.shape[2])
    product = jnp.dot(flat, weight.T, preferred_element_type=jnp.float32)
    return product.reshape(values.shape[0], values.shape[1], -1) * token_mask[:, :, None]


def reference(train_acts, train_cots, train_len, test_grads, proj_in, proj_out):
    positions = jnp.arange(SEQ, dtype=jnp.int32)
    token_mask = (positions[None, :] < train_len[:, None]).astype(jnp.float32)
    in_side = project_side(train_acts, proj_in, token_mask)
    out_side = project_side(train_cots, proj_out, token_mask)
    outer = jnp.einsum("esi,esj->eij", out_side, in_side, precision=lax.Precision.HIGHEST)
    train_grads = outer.reshape(outer.shape[0], K * K).astype(jnp.bfloat16)
    return jnp.dot(train_grads, test_grads.T, preferred_element_type=jnp.float32)
```

```python
import jax
import jax.numpy as jnp
from jax import lax
from jax.experimental import pallas as pl
from jax.experimental.pallas import tpu as pltpu
from jax.sharding import Mesh, PartitionSpec as P

GRP = ("x", "yh")
HID = ("z", "yl", "c")
SWAP = [(0, 1), (1, 0)]
STEPS = (1, -1, 3)
SIGNS = (1, -1)
BLOCK = 8 * 64 + 16
TOP = 14.0
VMEM = 32 * 1024 * 1024


def z_partner(z, step, sign):
    delta = STEPS[step] * sign
    return (z + (delta if z % 2 == 0 else -delta)) % 8


def along_z(array, step, sign):
    return lax.ppermute(array, "z", [(z, z_partner(z, step, sign)) for z in range(8)])


def in_hbm(array):
    return pltpu.with_memory_space_constraint(array, pltpu.HBM)


def owner_table():
    table = []
    for z in range(8):
        rows = []
        for sign in SIGNS:
            row = []
            for path in range(8):
                at = z
                for step in range(3):
                    if (path >> (2 - step)) & 1:
                        at = z_partner(at, step, sign)
                row.append(at)
            rows.append(row)
        table.append(rows)
    return table


def encode(values):
    top = jnp.max(jnp.abs(values), axis=1)
    power = jnp.ceil(jnp.log2(jnp.maximum(top, 1e-30)))
    codes = jnp.round(values * jnp.exp2(TOP - power)[:, None, :])
    tail = jnp.concatenate([power, jnp.zeros((8, 128), jnp.float32)], axis=0)
    whole = jnp.concatenate([codes.reshape(512, 128), tail], axis=0)
    return whole.astype(jnp.int32).astype(jnp.int16)


def decode(block):
    whole = block.astype(jnp.int32).astype(jnp.float32)
    power = whole[512:520]
    return whole[:512].reshape(8, 64, 128) * jnp.exp2(power - TOP)[:, None, :]


def scalar_table(z, core, lens):
    owner = jnp.asarray(owner_table(), jnp.int32).reshape(-1)
    return jnp.concatenate([jnp.stack([z, core]).astype(jnp.int32), owner, lens])


def owner_at(scalars, q, path):
    return scalars[2 + scalars[0] * 16 + q * 8 + path]


def project_kernel(flip, coded, scalars, acts, cots, proj_in, proj_out, *refs):
    outs, (acts_here, cots_here, in_here, out_here, sems, weight_sems) = refs[:2], refs[2:]
    core = scalars[1] ^ flip
    weights = [
        pltpu.make_async_copy(proj_in, in_here, weight_sems.at[0]),
        pltpu.make_async_copy(proj_out, out_here, weight_sems.at[1]),
    ]
    slots = [(q, path) for q in range(2) for path in range(8)]
    copies = []
    for slot, (q, path) in enumerate(slots):
        at = owner_at(scalars, q, path)
        copies.append(
            [
                pltpu.make_async_copy(acts.at[at, core, q], acts_here.at[slot], sems.at[slot, 0]),
                pltpu.make_async_copy(cots.at[at, core, q], cots_here.at[slot], sems.at[slot, 1]),
            ]
        )
    for pair in [weights] + copies:
        for copy in pair:
            copy.start()
    for copy in weights:
        copy.wait()
    zero = jnp.zeros((64, 128), jnp.bfloat16)
    weight = jnp.concatenate(
        [
            jnp.concatenate([out_here[...], zero], axis=1),
            jnp.concatenate([zero, in_here[...]], axis=1),
        ],
        axis=0,
    )
    rows = lax.broadcasted_iota(jnp.int32, (64, 128), 0)
    for slot, (q, path) in enumerate(slots):
        if slot % 4 == 0:
            for pair in copies[slot : slot + 4]:
                for copy in pair:
                    copy.wait()
        terms = lax.dot_general(
            jnp.concatenate([cots_here[slot], acts_here[slot]], axis=1),
            weight,
            (((1,), (1,)), ((), ())),
            preferred_element_type=jnp.float32,
        ).reshape(8, 64, 128)
        first = 130 + (owner_at(scalars, q, path) * 2 + core) * 16 + q * 8
        terms = jnp.stack([jnp.where(rows < scalars[first + e], terms[e], 0.0) for e in range(8)])
        outs[q][path] = encode(terms) if coded else terms


def project(flip, scalars, acts, cots, proj_in, proj_out, coded):
    if coded:
        shape = jax.ShapeDtypeStruct((8, BLOCK, 128), jnp.int16)
    else:
        shape = jax.ShapeDtypeStruct((8, 8, 64, 128), jnp.float32)

    def kernel(*refs):
        project_kernel(flip, coded, *refs)

    return pl.pallas_call(
        kernel,
        in_specs=[pl.BlockSpec(memory_space=pltpu.SMEM)] + [pl.BlockSpec(memory_space=pltpu.HBM)] * 4,
        out_specs=[pl.BlockSpec(memory_space=pltpu.VMEM)] * 2,
        out_shape=[shape] * 2,
        scratch_shapes=[
            pltpu.VMEM((16, 512, 128), jnp.bfloat16),
            pltpu.VMEM((16, 512, 128), jnp.bfloat16),
            pltpu.VMEM((64, 128), jnp.bfloat16),
            pltpu.VMEM((64, 128), jnp.bfloat16),
            pltpu.SemaphoreType.DMA((16, 2)),
            pltpu.SemaphoreType.DMA((2,)),
        ],
        compiler_params=pltpu.CompilerParams(vmem_limit_bytes=VMEM),
        name="project",
    )(scalars, *[in_hbm(a) for a in (acts, cots, proj_in, proj_out)])


def fold(kept, arrived, upper, coded):
    count = kept.shape[0] // 2
    first = count if upper else 0

    def kernel(kept_ref, arrived_ref, out_ref):
        total = kept_ref[0] + decode(arrived_ref[0])
        out_ref[0] = encode(total) if coded else total

    message = pl.BlockSpec((1, BLOCK, 128), lambda i: (i, 0, 0))
    plain = pl.BlockSpec((1, 8, 64, 128), lambda i: (i, 0, 0, 0))
    return pl.pallas_call(
        kernel,
        grid=(count,),
        in_specs=[
            pl.BlockSpec((1, 8, 64, 128), lambda i: (i + first, 0, 0, 0)),
            pl.BlockSpec((1, BLOCK, 128), lambda i: (i + first, 0, 0)),
        ],
        out_specs=message if coded else plain,
        out_shape=jax.ShapeDtypeStruct((count, BLOCK, 128), jnp.int16)
        if coded
        else jax.ShapeDtypeStruct((count, 8, 64, 128), jnp.float32),
        compiler_params=pltpu.CompilerParams(vmem_limit_bytes=VMEM),
        name="fold",
    )(kept, arrived)


def fold_both(kept, arrived):
    def kernel(kept_ref, arrived_ref, total_ref, coded_ref):
        total = kept_ref[0] + decode(arrived_ref[0])
        total_ref[0] = total
        coded_ref[0] = encode(total)

    return pl.pallas_call(
        kernel,
        out_shape=[
            jax.ShapeDtypeStruct((1, 8, 64, 128), jnp.float32),
            jax.ShapeDtypeStruct((1, BLOCK, 128), jnp.int16),
        ],
        compiler_params=pltpu.CompilerParams(vmem_limit_bytes=VMEM),
        name="fold_both",
    )(kept, arrived)


def outer_kernel(kept0, kept1, arrived0, arrived1, out_ref):
    for q, (kept, arrived) in enumerate(((kept0, arrived0), (kept1, arrived1))):
        total = kept[0] + decode(arrived[0])
        for e in range(8):
            outer = lax.dot_general(
                total[e, :, :64],
                total[e, :, 64:],
                (((0,), (0,)), ((), ())),
                precision=lax.Precision.HIGHEST,
                preferred_element_type=jnp.float32,
            )
            out_ref[q * 8 + e] = outer.astype(jnp.bfloat16)


def outer_grads(kept, arrived):
    return pl.pallas_call(
        outer_kernel,
        out_shape=jax.ShapeDtypeStruct((16, 64, 64), jnp.bfloat16),
        compiler_params=pltpu.CompilerParams(vmem_limit_bytes=VMEM),
        name="outer",
    )(*kept, *arrived)


def load_blocks(x, blocks, tests, sems):
    copies = []
    for n, (block, d, first) in enumerate(blocks):
        at = pl.multiple_of(lax.rem(x + d, 4) * 160 + first, 16)
        copies.append(pltpu.make_async_copy(block, tests.at[pl.ds(at, block.shape[0]), :], sems.at[n]))
    for copy in copies:
        copy.start()
    return copies


def place_grads(scalars, pieces, grads):
    for q in range(2):
        for side in range(2):
            for path in range(8):
                at = (owner_at(scalars, q, path) * 2 + (scalars[1] ^ side)) * 16
                rows = pl.ds(pl.multiple_of(at, 16), 16)
                grads[rows, q * 2048 : (q + 1) * 2048] = pieces[2 * q + side][path * 16 : path * 16 + 16, :]


def multiply(grads, tests, out):
    for first, last in ((0, 256), (256, 512), (512, 640)):
        out[:, first:last] = lax.dot_general(
            grads[...],
            tests[first:last, :],
            (((1,), (1,)), ((), ())),
            preferred_element_type=jnp.float32,
        )


def score_kernel(places, scalars, at_ref, *refs):
    pieces, blocks, refs = refs[:4], refs[4 : 4 + len(places)], refs[4 + len(places) :]
    out_ref, grads, tests, sems = refs
    copies = load_blocks(at_ref[0], [(b, *p) for b, p in zip(blocks, places)], tests, sems)
    place_grads(scalars, pieces, grads)
    for copy in copies:
        copy.wait()
    multiply(grads, tests, out_ref)


def finish_kernel(places, scalars, at_ref, *refs):
    pieces, blocks, refs = refs[:4], refs[4 : 4 + len(places)], refs[4 + len(places) :]
    own_ref, out_ref, grads, tests, sems, part = refs
    copies = load_blocks(at_ref[0], [(b, *p) for b, p in zip(blocks, places)], tests, sems)
    place_grads(scalars, pieces, grads)
    for copy in copies:
        copy.wait()
    multiply(grads, tests, part)
    flipped = at_ref[1] == 1
    own, other = own_ref[...], part[...]
    low, high = jnp.where(flipped, other, own), jnp.where(flipped, own, other)
    parts = []
    for x in range(4):
        parts += [low[:, x * 160 : x * 160 + 160], high[:, x * 160 : x * 160 + 160]]
    out_ref[...] = jnp.concatenate(parts, axis=1)


def score(scalars, at, pieces, blocks, own=None):
    places = [(d, first) for _, d, first in blocks]
    body = score_kernel if own is None else finish_kernel

    def kernel(*refs):
        body(places, *refs)

    whole = pl.BlockSpec(memory_space=pltpu.VMEM)
    scalar = pl.BlockSpec(memory_space=pltpu.SMEM)
    extra = [] if own is None else [own]
    scratch = [
        pltpu.VMEM((256, 4096), jnp.bfloat16),
        pltpu.VMEM((640, 4096), jnp.bfloat16),
        pltpu.SemaphoreType.DMA((len(blocks),)),
    ]
    if own is not None:
        scratch.append(pltpu.VMEM((256, 640), jnp.float32))
    return pl.pallas_call(
        kernel,
        in_specs=[scalar, scalar]
        + [whole] * 4
        + [pl.BlockSpec(memory_space=pltpu.HBM)] * len(blocks)
        + [whole] * len(extra),
        out_specs=whole,
        out_shape=jax.ShapeDtypeStruct((256, 640 if own is None else 1280), jnp.float32),
        scratch_shapes=scratch,
        compiler_params=pltpu.CompilerParams(vmem_limit_bytes=VMEM),
        name="score" if own is None else "finish",
    )(scalars, at, *pieces, *[in_hbm(block) for block, _, _ in blocks], *extra)


def local(train_acts, train_cots, train_len, test_grads, proj_in, proj_out):
    x, yh, z, core = (lax.axis_index(name) for name in ("x", "yh", "z", "c"))
    scalars = scalar_table(z, core, train_len)

    acts = train_acts.reshape(8, 2, 2, 512, 128)
    cots = train_cots.reshape(8, 2, 2, 512, 128)

    down = [(i, (i - 1) % 4) for i in range(4)]
    up = [(i, (i + 1) % 4) for i in range(4)]
    own1, own3 = lax.ppermute(test_grads, "x", down), lax.ppermute(test_grads, "x", up)
    other0 = lax.ppermute(test_grads, "yh", SWAP)

    away = project(1, scalars, acts, cots, proj_in, proj_out, True)
    arrived = [lax.ppermute(a, "c", SWAP) for a in away]
    kept = project(0, scalars, acts, cots, proj_in, proj_out, False)
    sent = [fold(k, a, True, True) for k, a in zip(kept, arrived)]
    moved = [along_z(a, 0, sign) for a, sign in zip(sent, SIGNS)]
    kept = [fold(k, a, False, False) for k, a in zip(kept, arrived)]
    arrived = moved

    for step in (1, 2):
        sent = [fold(k, a, True, True) for k, a in zip(kept, arrived)]
        moved = [along_z(a, step, sign) for a, sign in zip(sent, SIGNS)]
        kept = [fold(k, a, False, False) for k, a in zip(kept, arrived)]
        arrived = moved
        if step == 1:
            arrived, own1, own3, other0 = lax.optimization_barrier((arrived, own1, own3, other0))
            own2 = [lax.ppermute(own1[:80], "x", down), lax.ppermute(own3[80:], "x", up)]
    both = [fold_both(k, a) for k, a in zip(kept, arrived)]
    arrived = [lax.ppermute(coded, "yl", SWAP) for _, coded in both]
    arrived, own2 = lax.optimization_barrier((arrived, own2))
    other1, other3 = lax.ppermute(other0, "x", down), lax.ppermute(other0, "x", up)
    other2 = lax.ppermute(jnp.concatenate(own2, axis=0), "yh", SWAP)
    grads = outer_grads([total for total, _ in both], arrived).reshape(16, 4096)

    held = [grads[:, :2048], grads[:, 2048:]]
    for step in (2, 1, 0):
        got = [along_z(h, step, sign) for h, sign in zip(held, SIGNS)]
        held = [jnp.concatenate([h, g], axis=0) for h, g in zip(held, got)]
    pieces = [piece for h in held for piece in (h, lax.ppermute(h, "c", SWAP))]

    at = jnp.stack([x, yh])
    blocks = [(test_grads, 0, 0), (own1, 1, 0), (own3, 3, 0), (own2[0], 2, 0), (own2[1], 2, 80)]
    own = score(scalars, at, pieces, blocks)
    blocks = [(other0, 0, 0), (other1, 1, 0), (other2, 2, 0), (other3, 3, 0)]
    return score(scalars, at, pieces, blocks, own)


def solution(mesh):
    fine = Mesh(mesh.devices.reshape(4, 2, 8, 2, 2), ("x", "yh", "z", "yl", "c"))
    in_specs = (
        P(GRP, None, HID),
        P(GRP, None, HID),
        P(GRP),
        P(HID + GRP, None),
        P(None, HID),
        P(None, HID),
    )
    return jax.shard_map(local, mesh=fine, in_specs=in_specs, out_specs=P(GRP, HID), check_vma=False)
```

```python
import jax
import jax.numpy as jnp
from jax import lax
from jax.experimental import pallas as pl
from jax.experimental.pallas import tpu as pltpu
from jax.sharding import Mesh, PartitionSpec as P

GRP = ("x", "yh")
HID = ("z", "yl", "c")
SWAP = [(0, 1), (1, 0)]
STEPS = (1, -1, 3)
SIGNS = (1, -1)
BLOCK = 8 * 64 + 16
TOP = 14.0
VMEM = 32 * 1024 * 1024
SHORT = pl.CostEstimate(flops=0, bytes_accessed=0, transcendentals=0)


def z_partner(z, step, sign):
    delta = STEPS[step] * sign
    return (z + (delta if z % 2 == 0 else -delta)) % 8


def along_z(array, step, sign):
    return lax.ppermute(array, "z", [(z, z_partner(z, step, sign)) for z in range(8)])


def in_hbm(array):
    return pltpu.with_memory_space_constraint(array, pltpu.HBM)


def owner_table():
    table = []
    for z in range(8):
        rows = []
        for sign in SIGNS:
            row = []
            for path in range(8):
                at = z
                for step in range(3):
                    if (path >> (2 - step)) & 1:
                        at = z_partner(at, step, sign)
                row.append(at)
            rows.append(row)
        table.append(rows)
    return table


def encode(values):
    top = jnp.max(jnp.abs(values), axis=1)
    power = jnp.ceil(jnp.log2(jnp.maximum(top, 1e-30)))
    codes = jnp.round(values * jnp.exp2(TOP - power)[:, None, :])
    tail = jnp.concatenate([power, jnp.zeros((8, 128), jnp.float32)], axis=0)
    whole = jnp.concatenate([codes.reshape(512, 128), tail], axis=0)
    return whole.astype(jnp.int32).astype(jnp.int16)


def decode(block):
    whole = block.astype(jnp.int32).astype(jnp.float32)
    power = whole[512:520]
    return whole[:512].reshape(8, 64, 128) * jnp.exp2(power - TOP)[:, None, :]


def scalar_table(z, core, lens):
    owner = jnp.asarray(owner_table(), jnp.int32).reshape(-1)
    return jnp.concatenate([jnp.stack([z, core]).astype(jnp.int32), owner, lens])


def owner_at(scalars, q, path):
    return scalars[2 + scalars[0] * 16 + q * 8 + path]


def project_kernel(flip, coded, scalars, acts, cots, proj_in, proj_out, *refs):
    outs, (acts_here, cots_here, in_here, out_here, sems, weight_sems) = refs[:2], refs[2:]
    core = scalars[1] ^ flip
    weights = [
        pltpu.make_async_copy(proj_in, in_here, weight_sems.at[0]),
        pltpu.make_async_copy(proj_out, out_here, weight_sems.at[1]),
    ]
    slots = [(q, path) for q in range(2) for path in range(8)]
    copies = []
    for slot, (q, path) in enumerate(slots):
        at = owner_at(scalars, q, path)
        copies.append(
            [
                pltpu.make_async_copy(acts.at[at, core, q], acts_here.at[slot], sems.at[slot, 0]),
                pltpu.make_async_copy(cots.at[at, core, q], cots_here.at[slot], sems.at[slot, 1]),
            ]
        )
    for pair in [weights] + copies:
        for copy in pair:
            copy.start()
    for copy in weights:
        copy.wait()
    zero = jnp.zeros((64, 128), jnp.bfloat16)
    weight = jnp.concatenate(
        [
            jnp.concatenate([out_here[...], zero], axis=1),
            jnp.concatenate([zero, in_here[...]], axis=1),
        ],
        axis=0,
    )
    rows = lax.broadcasted_iota(jnp.int32, (64, 128), 0)
    for slot, (q, path) in enumerate(slots):
        if slot % 8 == 0:
            for pair in copies[slot : slot + 8]:
                for copy in pair:
                    copy.wait()
        terms = lax.dot_general(
            jnp.concatenate([cots_here[slot], acts_here[slot]], axis=1),
            weight,
            (((1,), (1,)), ((), ())),
            preferred_element_type=jnp.float32,
        ).reshape(8, 64, 128)
        first = 130 + (owner_at(scalars, q, path) * 2 + core) * 16 + q * 8
        terms = jnp.stack([jnp.where(rows < scalars[first + e], terms[e], 0.0) for e in range(8)])
        outs[q][path] = encode(terms) if coded else terms


def project(flip, scalars, acts, cots, proj_in, proj_out, coded):
    if coded:
        shape = jax.ShapeDtypeStruct((8, BLOCK, 128), jnp.int16)
    else:
        shape = jax.ShapeDtypeStruct((8, 8, 64, 128), jnp.float32)

    def kernel(*refs):
        project_kernel(flip, coded, *refs)

    return pl.pallas_call(
        kernel,
        in_specs=[pl.BlockSpec(memory_space=pltpu.SMEM)] + [pl.BlockSpec(memory_space=pltpu.HBM)] * 4,
        out_specs=[pl.BlockSpec(memory_space=pltpu.VMEM)] * 2,
        out_shape=[shape] * 2,
        scratch_shapes=[
            pltpu.VMEM((16, 512, 128), jnp.bfloat16),
            pltpu.VMEM((16, 512, 128), jnp.bfloat16),
            pltpu.VMEM((64, 128), jnp.bfloat16),
            pltpu.VMEM((64, 128), jnp.bfloat16),
            pltpu.SemaphoreType.DMA((16, 2)),
            pltpu.SemaphoreType.DMA((2,)),
        ],
        compiler_params=pltpu.CompilerParams(vmem_limit_bytes=VMEM),
        cost_estimate=SHORT,
        name="project",
    )(scalars, *[in_hbm(a) for a in (acts, cots, proj_in, proj_out)])


def fold(kept, arrived, upper, coded):
    count = kept.shape[0] // 2
    first = count if upper else 0

    def kernel(kept_ref, arrived_ref, out_ref):
        total = kept_ref[0] + decode(arrived_ref[0])
        out_ref[0] = encode(total) if coded else total

    message = pl.BlockSpec((1, BLOCK, 128), lambda i: (i, 0, 0))
    plain = pl.BlockSpec((1, 8, 64, 128), lambda i: (i, 0, 0, 0))
    return pl.pallas_call(
        kernel,
        grid=(count,),
        in_specs=[
            pl.BlockSpec((1, 8, 64, 128), lambda i: (i + first, 0, 0, 0)),
            pl.BlockSpec((1, BLOCK, 128), lambda i: (i + first, 0, 0)),
        ],
        out_specs=message if coded else plain,
        out_shape=jax.ShapeDtypeStruct((count, BLOCK, 128), jnp.int16)
        if coded
        else jax.ShapeDtypeStruct((count, 8, 64, 128), jnp.float32),
        compiler_params=pltpu.CompilerParams(vmem_limit_bytes=VMEM),
        cost_estimate=SHORT,
        name="fold",
    )(kept, arrived)


def fold_both(kept, arrived):
    def kernel(*refs):
        for q in range(2):
            total = refs[q][0] + decode(refs[2 + q][0])
            refs[4][q] = total
            refs[5][q] = encode(total)

    return pl.pallas_call(
        kernel,
        out_shape=[
            jax.ShapeDtypeStruct((2, 8, 64, 128), jnp.float32),
            jax.ShapeDtypeStruct((2, BLOCK, 128), jnp.int16),
        ],
        compiler_params=pltpu.CompilerParams(vmem_limit_bytes=VMEM),
        cost_estimate=SHORT,
        name="fold_both",
    )(*kept, *arrived)


def outer_kernel(kept, arrived, out_ref):
    for q in range(2):
        total = kept[q] + decode(arrived[q])
        for e in range(8):
            outer = lax.dot_general(
                total[e, :, :64],
                total[e, :, 64:],
                (((0,), (0,)), ((), ())),
                precision=lax.Precision.HIGHEST,
                preferred_element_type=jnp.float32,
            )
            out_ref[q * 8 + e] = outer.astype(jnp.bfloat16)


def outer_grads(kept, arrived):
    return pl.pallas_call(
        outer_kernel,
        out_shape=jax.ShapeDtypeStruct((16, 64, 64), jnp.bfloat16),
        compiler_params=pltpu.CompilerParams(vmem_limit_bytes=VMEM),
        cost_estimate=SHORT,
        name="outer",
    )(kept, arrived)


def load_tests(x, blocks, tests, sems):
    copies = []
    for n, (block, d, first) in enumerate(blocks):
        at = pl.multiple_of(lax.rem(x + d, 4) * 160 + first, 16)
        copies.append(pltpu.make_async_copy(block, tests.at[pl.ds(at, block.shape[0]), :], sems.at[n]))
    for copy in copies:
        copy.start()
    return copies


def place_grads(scalars, pieces, grads):
    for q in range(2):
        for side in range(2):
            for path in range(8):
                at = (owner_at(scalars, q, path) * 2 + (scalars[1] ^ side)) * 16
                rows = pl.ds(pl.multiple_of(at, 16), 16)
                grads[rows, q * 2048 : (q + 1) * 2048] = pieces[2 * q + side][path * 16 : path * 16 + 16, :]


def multiply(grads, tests, out):
    for first, last in ((0, 256), (256, 512), (512, 640)):
        out[:, first:last] = lax.dot_general(
            grads[...],
            tests[first:last, :],
            (((1,), (1,)), ((), ())),
            preferred_element_type=jnp.float32,
        )


def score_kernel(places, scalars, at_ref, *refs):
    pieces, blocks, refs = refs[:4], refs[4 : 4 + len(places)], refs[4 + len(places) :]
    out_ref, grads, tests, sems = refs
    copies = load_tests(at_ref[0], [(b, *p) for b, p in zip(blocks, places)], tests, sems)
    place_grads(scalars, pieces, grads)
    for copy in copies:
        copy.wait()
    multiply(grads, tests, out_ref)


def finish_kernel(places, scalars, at_ref, *refs):
    pieces, blocks, refs = refs[:4], refs[4 : 4 + len(places)], refs[4 + len(places) :]
    own_ref, out_ref, grads, tests, sems, part = refs
    copies = load_tests(at_ref[0], [(b, *p) for b, p in zip(blocks, places)], tests, sems)
    place_grads(scalars, pieces, grads)
    for copy in copies:
        copy.wait()
    multiply(grads, tests, part)
    flipped = at_ref[1] == 1
    own, other = own_ref[...], part[...]
    low, high = jnp.where(flipped, other, own), jnp.where(flipped, own, other)
    parts = []
    for x in range(4):
        parts += [low[:, x * 160 : x * 160 + 160], high[:, x * 160 : x * 160 + 160]]
    out_ref[...] = jnp.concatenate(parts, axis=1)


def score(scalars, at, pieces, blocks, own=None):
    places = [(d, first) for _, d, first in blocks]
    body = score_kernel if own is None else finish_kernel

    def kernel(*refs):
        body(places, *refs)

    whole = pl.BlockSpec(memory_space=pltpu.VMEM)
    scalar = pl.BlockSpec(memory_space=pltpu.SMEM)
    extra = [] if own is None else [own]
    scratch = [
        pltpu.VMEM((256, 4096), jnp.bfloat16),
        pltpu.VMEM((640, 4096), jnp.bfloat16),
        pltpu.SemaphoreType.DMA((len(blocks),)),
    ]
    if own is not None:
        scratch.append(pltpu.VMEM((256, 640), jnp.float32))
    return pl.pallas_call(
        kernel,
        in_specs=[scalar, scalar]
        + [whole] * 4
        + [pl.BlockSpec(memory_space=pltpu.HBM)] * len(blocks)
        + [whole] * len(extra),
        out_specs=whole,
        out_shape=jax.ShapeDtypeStruct((256, 640 if own is None else 1280), jnp.float32),
        scratch_shapes=scratch,
        compiler_params=pltpu.CompilerParams(vmem_limit_bytes=VMEM),
        cost_estimate=SHORT,
        name="score" if own is None else "finish",
    )(scalars, at, *pieces, *[in_hbm(block) for block, _, _ in blocks], *extra)


def local(train_acts, train_cots, train_len, test_grads, proj_in, proj_out):
    x, yh, z, core = (lax.axis_index(name) for name in ("x", "yh", "z", "c"))
    scalars = scalar_table(z, core, train_len)

    acts = train_acts.reshape(8, 2, 2, 512, 128)
    cots = train_cots.reshape(8, 2, 2, 512, 128)

    down = [(i, (i - 1) % 4) for i in range(4)]
    up = [(i, (i + 1) % 4) for i in range(4)]
    own1, own3 = lax.ppermute(test_grads, "x", down), lax.ppermute(test_grads, "x", up)
    other0 = lax.ppermute(test_grads, "yh", SWAP)

    away = project(1, scalars, acts, cots, proj_in, proj_out, True)
    arrived = [lax.ppermute(a, "c", SWAP) for a in away]
    kept = project(0, scalars, acts, cots, proj_in, proj_out, False)
    sent = [fold(k, a, True, True) for k, a in zip(kept, arrived)]
    moved = [along_z(a, 0, sign) for a, sign in zip(sent, SIGNS)]
    kept = [fold(k, a, False, False) for k, a in zip(kept, arrived)]
    arrived = moved

    for step in (1, 2):
        sent = [fold(k, a, True, True) for k, a in zip(kept, arrived)]
        moved = [along_z(a, step, sign) for a, sign in zip(sent, SIGNS)]
        kept = [fold(k, a, False, False) for k, a in zip(kept, arrived)]
        arrived = moved
    own2 = [lax.ppermute(own1[:80], "x", down), lax.ppermute(own3[80:], "x", up)]
    total, coded = fold_both(kept, arrived)
    arrived = lax.ppermute(coded, "yl", SWAP)
    arrived, own2 = lax.optimization_barrier((arrived, own2))
    other1, other3 = lax.ppermute(other0, "x", down), lax.ppermute(other0, "x", up)
    other2 = lax.ppermute(jnp.concatenate(own2, axis=0), "yh", SWAP)
    grads = outer_grads(total, arrived).reshape(16, 4096)

    held = [grads[:, :2048], grads[:, 2048:]]
    for step in (2, 1, 0):
        got = [along_z(h, step, sign) for h, sign in zip(held, SIGNS)]
        held = [jnp.concatenate([h, g], axis=0) for h, g in zip(held, got)]
    pieces = [piece for h in held for piece in (h, lax.ppermute(h, "c", SWAP))]

    at = jnp.stack([x, yh])
    blocks = [(test_grads, 0, 0), (own1, 1, 0), (own3, 3, 0), (own2[0], 2, 0), (own2[1], 2, 80)]
    own = score(scalars, at, pieces, blocks)
    blocks = [(other0, 0, 0), (other1, 1, 0), (other2, 2, 0), (other3, 3, 0)]
    return score(scalars, at, pieces, blocks, own)


def solution(mesh):
    fine = Mesh(mesh.devices.reshape(4, 2, 8, 2, 2), ("x", "yh", "z", "yl", "c"))
    in_specs = (
        P(GRP, None, HID),
        P(GRP, None, HID),
        P(GRP),
        P(HID + GRP, None),
        P(None, HID),
        P(None, HID),
    )
    return jax.shard_map(local, mesh=fine, in_specs=in_specs, out_specs=P(GRP, HID), check_vma=False)
```

```python
import jax
import jax.numpy as jnp
from jax import lax
from jax.experimental import pallas as pl
from jax.experimental.pallas import tpu as pltpu
from jax.sharding import Mesh, PartitionSpec as P

GRP = ("x", "yh")
HID = ("z", "yl", "c")
SWAP = [(0, 1), (1, 0)]
STEPS = (1, -1, 3)
SIGNS = (1, -1)
BLOCK = 8 * 64 + 16
TOP = 14.0
VMEM = 32 * 1024 * 1024
SHORT = pl.CostEstimate(flops=0, bytes_accessed=0, transcendentals=0)


def z_partner(z, step, sign):
    delta = STEPS[step] * sign
    return (z + (delta if z % 2 == 0 else -delta)) % 8


def along_z(array, step, sign):
    return lax.ppermute(array, "z", [(z, z_partner(z, step, sign)) for z in range(8)])


def in_hbm(array):
    return pltpu.with_memory_space_constraint(array, pltpu.HBM)


def owner_table():
    table = []
    for z in range(8):
        rows = []
        for sign in SIGNS:
            row = []
            for path in range(8):
                at = z
                for step in range(3):
                    if (path >> (2 - step)) & 1:
                        at = z_partner(at, step, sign)
                row.append(at)
            rows.append(row)
        table.append(rows)
    return table


def encode(values):
    top = jnp.max(jnp.abs(values), axis=1)
    power = jnp.ceil(jnp.log2(jnp.maximum(top, 1e-30)))
    codes = jnp.round(values * jnp.exp2(TOP - power)[:, None, :])
    tail = jnp.concatenate([power, jnp.zeros((8, 128), jnp.float32)], axis=0)
    whole = jnp.concatenate([codes.reshape(512, 128), tail], axis=0)
    return whole.astype(jnp.int32).astype(jnp.int16)


def decode(block):
    whole = block.astype(jnp.int32).astype(jnp.float32)
    power = whole[512:520]
    return whole[:512].reshape(8, 64, 128) * jnp.exp2(power - TOP)[:, None, :]


def scalar_table(z, core, lens):
    owner = jnp.asarray(owner_table(), jnp.int32).reshape(-1)
    return jnp.concatenate([jnp.stack([z, core]).astype(jnp.int32), owner, lens])


def owner_at(scalars, q, path):
    return scalars[2 + scalars[0] * 16 + q * 8 + path]


def project_kernel(flip, coded, scalars, acts, cots, proj_in, proj_out, *refs):
    outs, (acts_here, cots_here, in_here, out_here, sems, weight_sems) = refs[:2], refs[2:]
    core = scalars[1] ^ flip
    weights = [
        pltpu.make_async_copy(proj_in, in_here, weight_sems.at[0]),
        pltpu.make_async_copy(proj_out, out_here, weight_sems.at[1]),
    ]
    slots = [(q, path) for q in range(2) for path in range(8)]
    copies = []
    for slot, (q, path) in enumerate(slots):
        at = owner_at(scalars, q, path)
        copies.append(
            [
                pltpu.make_async_copy(acts.at[at, core, q], acts_here.at[slot], sems.at[slot, 0]),
                pltpu.make_async_copy(cots.at[at, core, q], cots_here.at[slot], sems.at[slot, 1]),
            ]
        )
    for pair in [weights] + copies:
        for copy in pair:
            copy.start()
    for copy in weights:
        copy.wait()
    zero = jnp.zeros((64, 128), jnp.bfloat16)
    weight = jnp.concatenate(
        [
            jnp.concatenate([out_here[...], zero], axis=1),
            jnp.concatenate([zero, in_here[...]], axis=1),
        ],
        axis=0,
    )
    rows = lax.broadcasted_iota(jnp.int32, (64, 128), 0)
    for slot, (q, path) in enumerate(slots):
        if slot % 8 == 0:
            for pair in copies[slot : slot + 8]:
                for copy in pair:
                    copy.wait()
        terms = lax.dot_general(
            jnp.concatenate([cots_here[slot], acts_here[slot]], axis=1),
            weight,
            (((1,), (1,)), ((), ())),
            preferred_element_type=jnp.float32,
        ).reshape(8, 64, 128)
        first = 130 + (owner_at(scalars, q, path) * 2 + core) * 16 + q * 8
        terms = jnp.stack([jnp.where(rows < scalars[first + e], terms[e], 0.0) for e in range(8)])
        outs[q][path] = encode(terms) if coded else terms


def project(flip, scalars, acts, cots, proj_in, proj_out, coded):
    if coded:
        shape = jax.ShapeDtypeStruct((8, BLOCK, 128), jnp.int16)
    else:
        shape = jax.ShapeDtypeStruct((8, 8, 64, 128), jnp.float32)

    def kernel(*refs):
        project_kernel(flip, coded, *refs)

    return pl.pallas_call(
        kernel,
        in_specs=[pl.BlockSpec(memory_space=pltpu.SMEM)] + [pl.BlockSpec(memory_space=pltpu.HBM)] * 4,
        out_specs=[pl.BlockSpec(memory_space=pltpu.VMEM)] * 2,
        out_shape=[shape] * 2,
        scratch_shapes=[
            pltpu.VMEM((16, 512, 128), jnp.bfloat16),
            pltpu.VMEM((16, 512, 128), jnp.bfloat16),
            pltpu.VMEM((64, 128), jnp.bfloat16),
            pltpu.VMEM((64, 128), jnp.bfloat16),
            pltpu.SemaphoreType.DMA((16, 2)),
            pltpu.SemaphoreType.DMA((2,)),
        ],
        compiler_params=pltpu.CompilerParams(vmem_limit_bytes=VMEM),
        cost_estimate=SHORT,
        name="project",
    )(scalars, *[in_hbm(a) for a in (acts, cots, proj_in, proj_out)])


def fold(kept, arrived, upper, coded):
    count = kept.shape[0] // 2
    first = count if upper else 0

    def kernel(kept_ref, arrived_ref, out_ref):
        total = kept_ref[0] + decode(arrived_ref[0])
        out_ref[0] = encode(total) if coded else total

    message = pl.BlockSpec((1, BLOCK, 128), lambda i: (i, 0, 0))
    plain = pl.BlockSpec((1, 8, 64, 128), lambda i: (i, 0, 0, 0))
    return pl.pallas_call(
        kernel,
        grid=(count,),
        in_specs=[
            pl.BlockSpec((1, 8, 64, 128), lambda i: (i + first, 0, 0, 0)),
            pl.BlockSpec((1, BLOCK, 128), lambda i: (i + first, 0, 0)),
        ],
        out_specs=message if coded else plain,
        out_shape=jax.ShapeDtypeStruct((count, BLOCK, 128), jnp.int16)
        if coded
        else jax.ShapeDtypeStruct((count, 8, 64, 128), jnp.float32),
        compiler_params=pltpu.CompilerParams(vmem_limit_bytes=VMEM),
        cost_estimate=SHORT,
        name="fold",
    )(kept, arrived)


def fold_both(kept, arrived):
    def kernel(*refs):
        for q in range(2):
            total = refs[q][0] + decode(refs[2 + q][0])
            refs[4][q] = total
            refs[5][q] = encode(total)

    return pl.pallas_call(
        kernel,
        out_shape=[
            jax.ShapeDtypeStruct((2, 8, 64, 128), jnp.float32),
            jax.ShapeDtypeStruct((2, BLOCK, 128), jnp.int16),
        ],
        compiler_params=pltpu.CompilerParams(vmem_limit_bytes=VMEM),
        cost_estimate=SHORT,
        name="fold_both",
    )(*kept, *arrived)


def outer_kernel(kept, arrived, out_ref):
    for q in range(2):
        total = kept[q] + decode(arrived[q])
        for e in range(8):
            outer = lax.dot_general(
                total[e, :, :64],
                total[e, :, 64:],
                (((0,), (0,)), ((), ())),
                precision=lax.Precision.HIGHEST,
                preferred_element_type=jnp.float32,
            )
            out_ref[q * 8 + e] = outer.astype(jnp.bfloat16)


def outer_grads(kept, arrived):
    return pl.pallas_call(
        outer_kernel,
        out_shape=jax.ShapeDtypeStruct((16, 64, 64), jnp.bfloat16),
        compiler_params=pltpu.CompilerParams(vmem_limit_bytes=VMEM),
        cost_estimate=SHORT,
        name="outer",
    )(kept, arrived)


def fetch_tests(x, blocks, tests, sems):
    for at in range(4):
        for block, d, first in blocks:

            @pl.when(lax.rem(x + d, 4) == at)
            def _():
                rows = pl.ds(at * 160 + first, block.shape[0])
                pltpu.make_async_copy(block, tests.at[rows, :], sems.at[at]).start()


def wait_tests(at, tests, sems):
    rows = tests.at[pl.ds(at * 160, 160), :]
    pltpu.make_async_copy(rows, rows, sems.at[at]).wait()


def times(grads, tests):
    return lax.dot_general(
        grads, tests, (((1,), (1,)), ((), ())), preferred_element_type=jnp.float32
    )


def score(scalars, at, pieces, own, other):
    blocks = own + other
    places = [(d, first) for _, d, first in blocks]

    def kernel(scalars, at_ref, *refs):
        pieces, blocks, refs = refs[:4], refs[4 : 4 + len(places)], refs[4 + len(places) :]
        own_ref, other_ref, grads, own_tests, other_tests, sems = refs
        x = at_ref[0]
        missing = lax.rem(x + 2, 4)
        blocks = [(block, *place) for block, place in zip(blocks, places)]
        fetch_tests(x, blocks[: len(own)], own_tests, sems.at[0])
        fetch_tests(x, blocks[len(own) :], other_tests, sems.at[1])
        other_tests[pl.ds(pl.multiple_of(missing * 160, 32), 160), :] = jnp.zeros((160, 4096), jnp.bfloat16)
        for q in range(2):
            for side in range(2):
                for path in range(8):
                    block = (owner_at(scalars, q, path) * 2 + (scalars[1] ^ side)) * 16
                    rows = pl.ds(pl.multiple_of(block, 16), 16)
                    grads[rows, q * 2048 : (q + 1) * 2048] = pieces[2 * q + side][path * 16 : path * 16 + 16, :]
        for first, last, needs in ((0, 256, (0, 1)), (256, 480, (2,)), (480, 640, (3,))):
            for block in needs:
                wait_tests(block, own_tests, sems.at[0])
            own_ref[:, first:last] = times(grads[...], own_tests[first:last, :])
        for block in range(4):

            @pl.when(missing != block)
            def _():
                wait_tests(block, other_tests, sems.at[1])

        for first, last in ((0, 256), (256, 512), (512, 640)):
            other_ref[:, first:last] = times(grads[...], other_tests[first:last, :])

    whole = pl.BlockSpec(memory_space=pltpu.VMEM)
    scalar = pl.BlockSpec(memory_space=pltpu.SMEM)
    return pl.pallas_call(
        kernel,
        in_specs=[scalar, scalar] + [whole] * 4 + [pl.BlockSpec(memory_space=pltpu.HBM)] * len(blocks),
        out_specs=[whole] * 3,
        out_shape=[
            jax.ShapeDtypeStruct((256, 640), jnp.float32),
            jax.ShapeDtypeStruct((256, 640), jnp.float32),
            jax.ShapeDtypeStruct((256, 4096), jnp.bfloat16),
        ],
        scratch_shapes=[
            pltpu.VMEM((640, 4096), jnp.bfloat16),
            pltpu.VMEM((640, 4096), jnp.bfloat16),
            pltpu.SemaphoreType.DMA((2, 4)),
        ],
        compiler_params=pltpu.CompilerParams(vmem_limit_bytes=VMEM),
        cost_estimate=SHORT,
        name="score",
    )(scalars, at, *pieces, *[in_hbm(block) for block, _, _ in blocks])


def finish(at, own, other, grads, far):
    def kernel(at_ref, own_ref, other_ref, grads, far_ref, out_ref):
        last = times(grads[...], far_ref[...])
        flipped = at_ref[1] == 1
        missing = lax.rem(at_ref[0] + 2, 4)
        parts = []
        for x in range(4):
            mine = own_ref[:, x * 160 : x * 160 + 160]
            theirs = jnp.where(missing == x, last, other_ref[:, x * 160 : x * 160 + 160])
            parts += [jnp.where(flipped, theirs, mine), jnp.where(flipped, mine, theirs)]
        out_ref[...] = jnp.concatenate(parts, axis=1)

    whole = pl.BlockSpec(memory_space=pltpu.VMEM)
    return pl.pallas_call(
        kernel,
        in_specs=[pl.BlockSpec(memory_space=pltpu.SMEM)] + [whole] * 4,
        out_specs=whole,
        out_shape=jax.ShapeDtypeStruct((256, 1280), jnp.float32),
        compiler_params=pltpu.CompilerParams(vmem_limit_bytes=VMEM),
        cost_estimate=SHORT,
        name="finish",
    )(at, own, other, grads, far)


def local(train_acts, train_cots, train_len, test_grads, proj_in, proj_out):
    x, yh, z, core = (lax.axis_index(name) for name in ("x", "yh", "z", "c"))
    scalars = scalar_table(z, core, train_len)

    acts = train_acts.reshape(8, 2, 2, 512, 128)
    cots = train_cots.reshape(8, 2, 2, 512, 128)

    away = project(1, scalars, acts, cots, proj_in, proj_out, True)
    arrived = [lax.ppermute(a, "c", SWAP) for a in away]
    kept = project(0, scalars, acts, cots, proj_in, proj_out, False)
    sent = [fold(k, a, True, True) for k, a in zip(kept, arrived)]
    moved = [along_z(a, 0, sign) for a, sign in zip(sent, SIGNS)]
    kept = [fold(k, a, False, False) for k, a in zip(kept, arrived)]
    arrived = moved

    down = [(i, (i - 1) % 4) for i in range(4)]
    up = [(i, (i + 1) % 4) for i in range(4)]
    own1, own3 = lax.ppermute(test_grads, "x", down), lax.ppermute(test_grads, "x", up)
    other0 = lax.ppermute(test_grads, "yh", SWAP)

    for step in (1, 2):
        sent = [fold(k, a, True, True) for k, a in zip(kept, arrived)]
        moved = [along_z(a, step, sign) for a, sign in zip(sent, SIGNS)]
        kept = [fold(k, a, False, False) for k, a in zip(kept, arrived)]
        arrived = moved
    own2 = [lax.ppermute(own1[:80], "x", down), lax.ppermute(own3[80:], "x", up)]
    total, coded = fold_both(kept, arrived)
    arrived = lax.ppermute(coded, "yl", SWAP)
    arrived, own2, other0 = lax.optimization_barrier((arrived, own2, other0))
    other1, other3 = lax.ppermute(other0, "x", down), lax.ppermute(other0, "x", up)
    other2 = lax.ppermute(jnp.concatenate(own2, axis=0), "yh", SWAP)
    grads = outer_grads(total, arrived).reshape(16, 4096)

    held = [grads[:, :2048], grads[:, 2048:]]
    for step in (2, 1, 0):
        got = [along_z(h, step, sign) for h, sign in zip(held, SIGNS)]
        held = [jnp.concatenate([h, g], axis=0) for h, g in zip(held, got)]
    pieces = [piece for h in held for piece in (h, lax.ppermute(h, "c", SWAP))]

    at = jnp.stack([x, yh])
    own = [(test_grads, 0, 0), (own1, 1, 0), (own3, 3, 0), (own2[0], 2, 0), (own2[1], 2, 80)]
    other = [(other0, 0, 0), (other1, 1, 0), (other3, 3, 0)]
    own, other, grads = score(scalars, at, pieces, own, other)
    return finish(at, own, other, grads, other2)


def solution(mesh):
    fine = Mesh(mesh.devices.reshape(4, 2, 8, 2, 2), ("x", "yh", "z", "yl", "c"))
    in_specs = (
        P(GRP, None, HID),
        P(GRP, None, HID),
        P(GRP),
        P(HID + GRP, None),
        P(None, HID),
        P(None, HID),
    )
    return jax.shard_map(local, mesh=fine, in_specs=in_specs, out_specs=P(GRP, HID), check_vma=False)
```

```python
import jax
import jax.numpy as jnp
from jax import lax
from jax.experimental import pallas as pl
from jax.experimental.pallas import tpu as pltpu
from jax.sharding import Mesh, PartitionSpec as P

GRP = ("x", "yh")
HID = ("z", "yl", "c")
SWAP = [(0, 1), (1, 0)]
STEPS = (1, -1, 3)
SIGNS = (1, -1)
BLOCK = 8 * 64 + 16
TOP = 14.0
VMEM = 32 * 1024 * 1024
SHORT = pl.CostEstimate(flops=0, bytes_accessed=0, transcendentals=0)


def z_partner(z, step, sign):
    delta = STEPS[step] * sign
    return (z + (delta if z % 2 == 0 else -delta)) % 8


def along_z(array, step, sign):
    return lax.ppermute(array, "z", [(z, z_partner(z, step, sign)) for z in range(8)])


def in_hbm(array):
    return pltpu.with_memory_space_constraint(array, pltpu.HBM)


def owner_table():
    table = []
    for z in range(8):
        rows = []
        for sign in SIGNS:
            row = []
            for path in range(8):
                at = z
                for step in range(3):
                    if (path >> (2 - step)) & 1:
                        at = z_partner(at, step, sign)
                row.append(at)
            rows.append(row)
        table.append(rows)
    return table


def encode(values):
    top = jnp.max(jnp.abs(values), axis=1)
    power = jnp.ceil(jnp.log2(jnp.maximum(top, 1e-30)))
    codes = jnp.round(values * jnp.exp2(TOP - power)[:, None, :])
    tail = jnp.concatenate([power, jnp.zeros((8, 128), jnp.float32)], axis=0)
    whole = jnp.concatenate([codes.reshape(512, 128), tail], axis=0)
    return whole.astype(jnp.int32).astype(jnp.int16)


def decode(block):
    whole = block.astype(jnp.int32).astype(jnp.float32)
    power = whole[512:520]
    return whole[:512].reshape(8, 64, 128) * jnp.exp2(power - TOP)[:, None, :]


def scalar_table(z, core, lens):
    owner = jnp.asarray(owner_table(), jnp.int32).reshape(-1)
    return jnp.concatenate([jnp.stack([z, core]).astype(jnp.int32), owner, lens])


def owner_at(scalars, q, path):
    return scalars[2 + scalars[0] * 16 + q * 8 + path]


def project_kernel(flip, coded, scalars, acts, cots, proj_in, proj_out, *refs):
    outs, (acts_here, cots_here, in_here, out_here, sems, weight_sems) = refs[:2], refs[2:]
    core = scalars[1] ^ flip
    weights = [
        pltpu.make_async_copy(proj_in, in_here, weight_sems.at[0]),
        pltpu.make_async_copy(proj_out, out_here, weight_sems.at[1]),
    ]
    slots = [(q, path) for q in range(2) for path in range(8)]
    copies = []
    for slot, (q, path) in enumerate(slots):
        at = owner_at(scalars, q, path)
        copies.append(
            [
                pltpu.make_async_copy(acts.at[at, core, q], acts_here.at[slot], sems.at[slot, 0]),
                pltpu.make_async_copy(cots.at[at, core, q], cots_here.at[slot], sems.at[slot, 1]),
            ]
        )
    for pair in [weights] + copies:
        for copy in pair:
            copy.start()
    for copy in weights:
        copy.wait()
    zero = jnp.zeros((64, 128), jnp.bfloat16)
    weight = jnp.concatenate(
        [
            jnp.concatenate([out_here[...], zero], axis=1),
            jnp.concatenate([zero, in_here[...]], axis=1),
        ],
        axis=0,
    )
    rows = lax.broadcasted_iota(jnp.int32, (64, 128), 0)
    for slot, (q, path) in enumerate(slots):
        if slot % 8 == 0:
            for pair in copies[slot : slot + 8]:
                for copy in pair:
                    copy.wait()
        terms = lax.dot_general(
            jnp.concatenate([cots_here[slot], acts_here[slot]], axis=1),
            weight,
            (((1,), (1,)), ((), ())),
            preferred_element_type=jnp.float32,
        ).reshape(8, 64, 128)
        first = 130 + (owner_at(scalars, q, path) * 2 + core) * 16 + q * 8
        terms = jnp.stack([jnp.where(rows < scalars[first + e], terms[e], 0.0) for e in range(8)])
        outs[q][path] = encode(terms) if coded else terms


def project(flip, scalars, acts, cots, proj_in, proj_out, coded):
    if coded:
        shape = jax.ShapeDtypeStruct((8, BLOCK, 128), jnp.int16)
    else:
        shape = jax.ShapeDtypeStruct((8, 8, 64, 128), jnp.float32)

    def kernel(*refs):
        project_kernel(flip, coded, *refs)

    return pl.pallas_call(
        kernel,
        in_specs=[pl.BlockSpec(memory_space=pltpu.SMEM)] + [pl.BlockSpec(memory_space=pltpu.HBM)] * 4,
        out_specs=[pl.BlockSpec(memory_space=pltpu.VMEM)] * 2,
        out_shape=[shape] * 2,
        scratch_shapes=[
            pltpu.VMEM((16, 512, 128), jnp.bfloat16),
            pltpu.VMEM((16, 512, 128), jnp.bfloat16),
            pltpu.VMEM((64, 128), jnp.bfloat16),
            pltpu.VMEM((64, 128), jnp.bfloat16),
            pltpu.SemaphoreType.DMA((16, 2)),
            pltpu.SemaphoreType.DMA((2,)),
        ],
        compiler_params=pltpu.CompilerParams(vmem_limit_bytes=VMEM),
        cost_estimate=SHORT,
        name="project",
    )(scalars, *[in_hbm(a) for a in (acts, cots, proj_in, proj_out)])


def fold(kept, arrived, upper, coded):
    count = kept.shape[0] // 2
    first = count if upper else 0

    def kernel(kept_ref, arrived_ref, out_ref):
        total = kept_ref[0] + decode(arrived_ref[0])
        out_ref[0] = encode(total) if coded else total

    message = pl.BlockSpec((1, BLOCK, 128), lambda i: (i, 0, 0))
    plain = pl.BlockSpec((1, 8, 64, 128), lambda i: (i, 0, 0, 0))
    return pl.pallas_call(
        kernel,
        grid=(count,),
        in_specs=[
            pl.BlockSpec((1, 8, 64, 128), lambda i: (i + first, 0, 0, 0)),
            pl.BlockSpec((1, BLOCK, 128), lambda i: (i + first, 0, 0)),
        ],
        out_specs=message if coded else plain,
        out_shape=jax.ShapeDtypeStruct((count, BLOCK, 128), jnp.int16)
        if coded
        else jax.ShapeDtypeStruct((count, 8, 64, 128), jnp.float32),
        compiler_params=pltpu.CompilerParams(vmem_limit_bytes=VMEM),
        cost_estimate=SHORT,
        name="fold",
    )(kept, arrived)


def fold_both(kept, arrived):
    def kernel(*refs):
        for q in range(2):
            total = refs[q][0] + decode(refs[2 + q][0])
            refs[4][q] = total
            refs[5][q] = encode(total)

    return pl.pallas_call(
        kernel,
        out_shape=[
            jax.ShapeDtypeStruct((2, 8, 64, 128), jnp.float32),
            jax.ShapeDtypeStruct((2, BLOCK, 128), jnp.int16),
        ],
        compiler_params=pltpu.CompilerParams(vmem_limit_bytes=VMEM),
        cost_estimate=SHORT,
        name="fold_both",
    )(*kept, *arrived)


def outer_kernel(kept, arrived, out_ref):
    for q in range(2):
        total = kept[q] + decode(arrived[q])
        for e in range(8):
            outer = lax.dot_general(
                total[e, :, :64],
                total[e, :, 64:],
                (((0,), (0,)), ((), ())),
                precision=lax.Precision.HIGHEST,
                preferred_element_type=jnp.float32,
            )
            out_ref[q * 8 + e] = outer.astype(jnp.bfloat16)


def outer_grads(kept, arrived):
    return pl.pallas_call(
        outer_kernel,
        out_shape=jax.ShapeDtypeStruct((16, 64, 64), jnp.bfloat16),
        compiler_params=pltpu.CompilerParams(vmem_limit_bytes=VMEM),
        cost_estimate=SHORT,
        name="outer",
    )(kept, arrived)


def fetch_tests(x, blocks, tests, sems):
    for at in range(4):
        for block, d, first in blocks:

            @pl.when(lax.rem(x + d, 4) == at)
            def _():
                rows = pl.ds(at * 160 + first, block.shape[0])
                pltpu.make_async_copy(block, tests.at[rows, :], sems.at[at]).start()


def wait_tests(at, tests, sems):
    rows = tests.at[pl.ds(at * 160, 160), :]
    pltpu.make_async_copy(rows, rows, sems.at[at]).wait()


def times(grads, tests):
    return lax.dot_general(
        grads, tests, (((1,), (1,)), ((), ())), preferred_element_type=jnp.float32
    )


def score(scalars, at, pieces, own, other):
    blocks = own + other
    places = [(d, first) for _, d, first in blocks]

    def kernel(scalars, at_ref, *refs):
        pieces, blocks, refs = refs[:4], refs[4 : 4 + len(places)], refs[4 + len(places) :]
        own_ref, other_ref, grads, own_tests, other_tests, sems = refs
        x = at_ref[0]
        missing = lax.rem(x + 2, 4)
        blocks = [(block, *place) for block, place in zip(blocks, places)]
        fetch_tests(x, blocks[: len(own)], own_tests, sems.at[0])
        fetch_tests(x, blocks[len(own) :], other_tests, sems.at[1])
        other_tests[pl.ds(pl.multiple_of(missing * 160, 32), 160), :] = jnp.zeros((160, 4096), jnp.bfloat16)
        for q in range(2):
            for side in range(2):
                for path in range(8):
                    block = (owner_at(scalars, q, path) * 2 + (scalars[1] ^ side)) * 16
                    rows = pl.ds(pl.multiple_of(block, 16), 16)
                    grads[rows, q * 2048 : (q + 1) * 2048] = pieces[2 * q + side][path * 16 : path * 16 + 16, :]
        for first, last, needs in ((0, 256, (0, 1)), (256, 480, (2,)), (480, 640, (3,))):
            for block in needs:
                wait_tests(block, own_tests, sems.at[0])
            own_ref[:, first:last] = times(grads[...], own_tests[first:last, :])
        for block in range(4):

            @pl.when(missing != block)
            def _():
                wait_tests(block, other_tests, sems.at[1])

        for first, last in ((0, 256), (256, 512), (512, 640)):
            other_ref[:, first:last] = times(grads[...], other_tests[first:last, :])

    whole = pl.BlockSpec(memory_space=pltpu.VMEM)
    scalar = pl.BlockSpec(memory_space=pltpu.SMEM)
    return pl.pallas_call(
        kernel,
        in_specs=[scalar, scalar] + [whole] * 4 + [pl.BlockSpec(memory_space=pltpu.HBM)] * len(blocks),
        out_specs=[whole] * 3,
        out_shape=[
            jax.ShapeDtypeStruct((256, 640), jnp.float32),
            jax.ShapeDtypeStruct((256, 640), jnp.float32),
            jax.ShapeDtypeStruct((256, 4096), jnp.bfloat16),
        ],
        scratch_shapes=[
            pltpu.VMEM((640, 4096), jnp.bfloat16),
            pltpu.VMEM((640, 4096), jnp.bfloat16),
            pltpu.SemaphoreType.DMA((2, 4)),
        ],
        compiler_params=pltpu.CompilerParams(vmem_limit_bytes=VMEM),
        cost_estimate=SHORT,
        name="score",
    )(scalars, at, *pieces, *[in_hbm(block) for block, _, _ in blocks])


def finish(at, own, other, grads, far):
    def kernel(at_ref, own_ref, other_ref, grads, far_ref, out_ref):
        last = times(grads[...], far_ref[...])
        flipped = at_ref[1] == 1
        missing = lax.rem(at_ref[0] + 2, 4)
        parts = []
        for x in range(4):
            mine = own_ref[:, x * 160 : x * 160 + 160]
            theirs = jnp.where(missing == x, last, other_ref[:, x * 160 : x * 160 + 160])
            parts += [jnp.where(flipped, theirs, mine), jnp.where(flipped, mine, theirs)]
        out_ref[...] = jnp.concatenate(parts, axis=1)

    whole = pl.BlockSpec(memory_space=pltpu.VMEM)
    return pl.pallas_call(
        kernel,
        in_specs=[pl.BlockSpec(memory_space=pltpu.SMEM)] + [whole] * 4,
        out_specs=whole,
        out_shape=jax.ShapeDtypeStruct((256, 1280), jnp.float32),
        compiler_params=pltpu.CompilerParams(vmem_limit_bytes=VMEM),
        cost_estimate=SHORT,
        name="finish",
    )(at, own, other, grads, far)


def local(train_acts, train_cots, train_len, test_grads, proj_in, proj_out):
    x, yh, z, core = (lax.axis_index(name) for name in ("x", "yh", "z", "c"))
    scalars = scalar_table(z, core, train_len)

    acts = train_acts.reshape(8, 2, 2, 512, 128)
    cots = train_cots.reshape(8, 2, 2, 512, 128)

    away = project(1, scalars, acts, cots, proj_in, proj_out, True)
    arrived = [lax.ppermute(a, "c", SWAP) for a in away]
    kept = project(0, scalars, acts, cots, proj_in, proj_out, False)
    sent = [fold(k, a, True, True) for k, a in zip(kept, arrived)]
    moved = [along_z(a, 0, sign) for a, sign in zip(sent, SIGNS)]
    kept = [fold(k, a, False, False) for k, a in zip(kept, arrived)]
    arrived = moved

    down = [(i, (i - 1) % 4) for i in range(4)]
    up = [(i, (i + 1) % 4) for i in range(4)]
    own1, own3 = lax.ppermute(test_grads, "x", down), lax.ppermute(test_grads, "x", up)
    other0 = lax.ppermute(test_grads, "yh", SWAP)

    for step in (1, 2):
        sent = [fold(k, a, True, True) for k, a in zip(kept, arrived)]
        moved = [along_z(a, step, sign) for a, sign in zip(sent, SIGNS)]
        kept = [fold(k, a, False, False) for k, a in zip(kept, arrived)]
        arrived = moved
    own2 = [lax.ppermute(own1[:80], "x", down), lax.ppermute(own3[80:], "x", up)]
    total, coded = fold_both(kept, arrived)
    arrived = lax.ppermute(coded, "yl", SWAP)
    arrived, own2 = lax.optimization_barrier((arrived, own2))
    other1, other3 = lax.ppermute(other0, "x", down), lax.ppermute(other0, "x", up)
    other2 = lax.ppermute(jnp.concatenate(own2, axis=0), "yh", SWAP)
    grads = outer_grads(total, arrived).reshape(16, 4096)

    held = [grads[:, :2048], grads[:, 2048:]]
    for step in (2, 1, 0):
        got = [along_z(h, step, sign) for h, sign in zip(held, SIGNS)]
        held = [jnp.concatenate([h, g], axis=0) for h, g in zip(held, got)]
    pieces = [piece for h in held for piece in (h, lax.ppermute(h, "c", SWAP))]

    at = jnp.stack([x, yh])
    own = [(test_grads, 0, 0), (own1, 1, 0), (own3, 3, 0), (own2[0], 2, 0), (own2[1], 2, 80)]
    other = [(other0, 0, 0), (other1, 1, 0), (other3, 3, 0)]
    own, other, grads = score(scalars, at, pieces, own, other)
    return finish(at, own, other, grads, other2)


def solution(mesh):
    fine = Mesh(mesh.devices.reshape(4, 2, 8, 2, 2), ("x", "yh", "z", "yl", "c"))
    in_specs = (
        P(GRP, None, HID),
        P(GRP, None, HID),
        P(GRP),
        P(HID + GRP, None),
        P(None, HID),
        P(None, HID),
    )
    return jax.shard_map(local, mesh=fine, in_specs=in_specs, out_specs=P(GRP, HID), check_vma=False)
```

```python
import jax
import jax.numpy as jnp
from jax import lax
from jax.experimental import pallas as pl
from jax.experimental.pallas import tpu as pltpu
from jax.sharding import Mesh, PartitionSpec as P

GRP = ("x", "yh")
HID = ("z", "yl", "c")
SWAP = [(0, 1), (1, 0)]
STEPS = (1, -1)
SIGNS = (1, -1)
BLOCK = 8 * 64 + 16
TOP = 14.0
VMEM = 32 * 1024 * 1024
SHORT = pl.CostEstimate(flops=0, bytes_accessed=0, transcendentals=0)


def z_partner(z, step, sign):
    if step == 2:
        return (z + 4) % 8
    delta = STEPS[step] * sign
    return (z + (delta if z % 2 == 0 else -delta)) % 8


def along_z(array, step, sign):
    return lax.ppermute(array, "z", [(z, z_partner(z, step, sign)) for z in range(8)])


def in_hbm(array):
    return pltpu.with_memory_space_constraint(array, pltpu.HBM)


def owner_table():
    table = []
    for z in range(8):
        rows = []
        for sign in SIGNS:
            row = []
            for path in range(8):
                at = z
                for step in range(3):
                    if (path >> (2 - step)) & 1:
                        at = z_partner(at, step, sign)
                row.append(at)
            rows.append(row)
        table.append(rows)
    return table


def encode(values):
    top = jnp.max(jnp.abs(values), axis=1)
    power = jnp.ceil(jnp.log2(jnp.maximum(top, 1e-30)))
    codes = jnp.round(values * jnp.exp2(TOP - power)[:, None, :])
    tail = jnp.concatenate([power, jnp.zeros((8, 128), jnp.float32)], axis=0)
    whole = jnp.concatenate([codes.reshape(512, 128), tail], axis=0)
    return whole.astype(jnp.int32).astype(jnp.int16)


def decode(block):
    whole = block.astype(jnp.int32).astype(jnp.float32)
    power = whole[512:520]
    return whole[:512].reshape(8, 64, 128) * jnp.exp2(power - TOP)[:, None, :]


def scalar_table(z, core, lens):
    owner = jnp.asarray(owner_table(), jnp.int32).reshape(-1)
    return jnp.concatenate([jnp.stack([z, core]).astype(jnp.int32), owner, lens])


def owner_at(scalars, q, path):
    return scalars[2 + scalars[0] * 16 + q * 8 + path]


def project_kernel(flip, coded, scalars, acts, cots, proj_in, proj_out, *refs):
    outs, (acts_here, cots_here, in_here, out_here, sems, weight_sems) = refs[:2], refs[2:]
    core = scalars[1] ^ flip
    weights = [
        pltpu.make_async_copy(proj_in, in_here, weight_sems.at[0]),
        pltpu.make_async_copy(proj_out, out_here, weight_sems.at[1]),
    ]
    slots = [(q, path) for q in range(2) for path in range(8)]
    copies = []
    for slot, (q, path) in enumerate(slots):
        at = owner_at(scalars, q, path)
        copies.append(
            [
                pltpu.make_async_copy(acts.at[at, core, q], acts_here.at[slot], sems.at[slot, 0]),
                pltpu.make_async_copy(cots.at[at, core, q], cots_here.at[slot], sems.at[slot, 1]),
            ]
        )
    for pair in [weights] + copies:
        for copy in pair:
            copy.start()
    for copy in weights:
        copy.wait()
    zero = jnp.zeros((64, 128), jnp.bfloat16)
    weight = jnp.concatenate(
        [
            jnp.concatenate([out_here[...], zero], axis=1),
            jnp.concatenate([zero, in_here[...]], axis=1),
        ],
        axis=0,
    )
    rows = lax.broadcasted_iota(jnp.int32, (64, 128), 0)
    for slot, (q, path) in enumerate(slots):
        if slot % 8 == 0:
            for pair in copies[slot : slot + 8]:
                for copy in pair:
                    copy.wait()
        terms = lax.dot_general(
            jnp.concatenate([cots_here[slot], acts_here[slot]], axis=1),
            weight,
            (((1,), (1,)), ((), ())),
            preferred_element_type=jnp.float32,
        ).reshape(8, 64, 128)
        first = 130 + (owner_at(scalars, q, path) * 2 + core) * 16 + q * 8
        terms = jnp.stack([jnp.where(rows < scalars[first + e], terms[e], 0.0) for e in range(8)])
        outs[q][path] = encode(terms) if coded else terms


def project(flip, scalars, acts, cots, proj_in, proj_out, coded):
    if coded:
        shape = jax.ShapeDtypeStruct((8, BLOCK, 128), jnp.int16)
    else:
        shape = jax.ShapeDtypeStruct((8, 8, 64, 128), jnp.float32)

    def kernel(*refs):
        project_kernel(flip, coded, *refs)

    return pl.pallas_call(
        kernel,
        in_specs=[pl.BlockSpec(memory_space=pltpu.SMEM)] + [pl.BlockSpec(memory_space=pltpu.HBM)] * 4,
        out_specs=[pl.BlockSpec(memory_space=pltpu.VMEM)] * 2,
        out_shape=[shape] * 2,
        scratch_shapes=[
            pltpu.VMEM((16, 512, 128), jnp.bfloat16),
            pltpu.VMEM((16, 512, 128), jnp.bfloat16),
            pltpu.VMEM((64, 128), jnp.bfloat16),
            pltpu.VMEM((64, 128), jnp.bfloat16),
            pltpu.SemaphoreType.DMA((16, 2)),
            pltpu.SemaphoreType.DMA((2,)),
        ],
        compiler_params=pltpu.CompilerParams(vmem_limit_bytes=VMEM),
        cost_estimate=SHORT,
        name="project",
    )(scalars, *[in_hbm(a) for a in (acts, cots, proj_in, proj_out)])


def fold(kept, arrived, upper, coded):
    count = kept.shape[0] // 2
    first = count if upper else 0

    def kernel(kept_ref, arrived_ref, out_ref):
        total = kept_ref[0] + decode(arrived_ref[0])
        out_ref[0] = encode(total) if coded else total

    message = pl.BlockSpec((1, BLOCK, 128), lambda i: (i, 0, 0))
    plain = pl.BlockSpec((1, 8, 64, 128), lambda i: (i, 0, 0, 0))
    return pl.pallas_call(
        kernel,
        grid=(count,),
        in_specs=[
            pl.BlockSpec((1, 8, 64, 128), lambda i: (i + first, 0, 0, 0)),
            pl.BlockSpec((1, BLOCK, 128), lambda i: (i + first, 0, 0)),
        ],
        out_specs=message if coded else plain,
        out_shape=jax.ShapeDtypeStruct((count, BLOCK, 128), jnp.int16)
        if coded
        else jax.ShapeDtypeStruct((count, 8, 64, 128), jnp.float32),
        compiler_params=pltpu.CompilerParams(vmem_limit_bytes=VMEM),
        cost_estimate=SHORT,
        name="fold",
    )(kept, arrived)


def fold_pair(kept, arrived):
    def kernel(*refs):
        for q in range(2):
            refs[4][q] = encode(refs[q][1] + decode(refs[2 + q][1]))
            refs[5][q] = refs[q][0] + decode(refs[2 + q][0])

    return pl.pallas_call(
        kernel,
        out_shape=[
            jax.ShapeDtypeStruct((2, BLOCK, 128), jnp.int16),
            jax.ShapeDtypeStruct((2, 8, 64, 128), jnp.float32),
        ],
        compiler_params=pltpu.CompilerParams(vmem_limit_bytes=VMEM),
        cost_estimate=SHORT,
        name="fold_pair",
    )(*kept, *arrived)


def fold_both(kept, arrived):
    def kernel(kept_ref, arrived_ref, total_ref, coded_ref):
        for q in range(2):
            total = kept_ref[q] + decode(arrived_ref[q])
            total_ref[q] = total
            coded_ref[q] = encode(total)

    return pl.pallas_call(
        kernel,
        out_shape=[
            jax.ShapeDtypeStruct((2, 8, 64, 128), jnp.float32),
            jax.ShapeDtypeStruct((2, BLOCK, 128), jnp.int16),
        ],
        compiler_params=pltpu.CompilerParams(vmem_limit_bytes=VMEM),
        cost_estimate=SHORT,
        name="fold_both",
    )(kept, arrived)


def outer_kernel(kept, arrived, out_ref):
    for q in range(2):
        total = kept[q] + decode(arrived[q])
        for e in range(8):
            outer = lax.dot_general(
                total[e, :, :64],
                total[e, :, 64:],
                (((0,), (0,)), ((), ())),
                precision=lax.Precision.HIGHEST,
                preferred_element_type=jnp.float32,
            )
            out_ref[q * 8 + e] = outer.astype(jnp.bfloat16)


def outer_grads(kept, arrived):
    return pl.pallas_call(
        outer_kernel,
        out_shape=jax.ShapeDtypeStruct((16, 64, 64), jnp.bfloat16),
        compiler_params=pltpu.CompilerParams(vmem_limit_bytes=VMEM),
        cost_estimate=SHORT,
        name="outer",
    )(kept, arrived)


def fetch_tests(x, blocks, tests, sems):
    for at in range(4):
        for block, d, first in blocks:

            @pl.when(lax.rem(x + d, 4) == at)
            def _():
                rows = pl.ds(at * 160 + first, block.shape[0])
                pltpu.make_async_copy(block, tests.at[rows, :], sems.at[at]).start()


def wait_tests(at, tests, sems):
    rows = tests.at[pl.ds(at * 160, 160), :]
    pltpu.make_async_copy(rows, rows, sems.at[at]).wait()


def times(grads, tests):
    return lax.dot_general(
        grads, tests, (((1,), (1,)), ((), ())), preferred_element_type=jnp.float32
    )


def score(scalars, at, pieces, own, other):
    blocks = own + other
    places = [(d, first) for _, d, first in blocks]

    def kernel(scalars, at_ref, *refs):
        pieces, blocks, refs = refs[:4], refs[4 : 4 + len(places)], refs[4 + len(places) :]
        own_ref, other_ref, grads, own_tests, other_tests, sems = refs
        x = at_ref[0]
        missing = lax.rem(x + 2, 4)
        blocks = [(block, *place) for block, place in zip(blocks, places)]
        fetch_tests(x, blocks[: len(own)], own_tests, sems.at[0])
        fetch_tests(x, blocks[len(own) :], other_tests, sems.at[1])
        other_tests[pl.ds(pl.multiple_of(missing * 160, 32), 160), :] = jnp.zeros((160, 4096), jnp.bfloat16)
        for q in range(2):
            for side in range(2):
                for path in range(8):
                    block = (owner_at(scalars, q, path) * 2 + (scalars[1] ^ side)) * 16
                    rows = pl.ds(pl.multiple_of(block, 16), 16)
                    grads[rows, q * 2048 : (q + 1) * 2048] = pieces[2 * q + side][path * 16 : path * 16 + 16, :]
        for first, last, needs in ((0, 256, (0, 1)), (256, 480, (2,)), (480, 640, (3,))):
            for block in needs:
                wait_tests(block, own_tests, sems.at[0])
            own_ref[:, first:last] = times(grads[...], own_tests[first:last, :])
        for block in range(4):

            @pl.when(missing != block)
            def _():
                wait_tests(block, other_tests, sems.at[1])

        for first, last in ((0, 256), (256, 512), (512, 640)):
            other_ref[:, first:last] = times(grads[...], other_tests[first:last, :])

    whole = pl.BlockSpec(memory_space=pltpu.VMEM)
    scalar = pl.BlockSpec(memory_space=pltpu.SMEM)
    return pl.pallas_call(
        kernel,
        in_specs=[scalar, scalar] + [whole] * 4 + [pl.BlockSpec(memory_space=pltpu.HBM)] * len(blocks),
        out_specs=[whole] * 3,
        out_shape=[
            jax.ShapeDtypeStruct((256, 640), jnp.float32),
            jax.ShapeDtypeStruct((256, 640), jnp.float32),
            jax.ShapeDtypeStruct((256, 4096), jnp.bfloat16),
        ],
        scratch_shapes=[
            pltpu.VMEM((640, 4096), jnp.bfloat16),
            pltpu.VMEM((640, 4096), jnp.bfloat16),
            pltpu.SemaphoreType.DMA((2, 4)),
        ],
        compiler_params=pltpu.CompilerParams(vmem_limit_bytes=VMEM),
        cost_estimate=SHORT,
        name="score",
    )(scalars, at, *pieces, *[in_hbm(block) for block, _, _ in blocks])


def finish(at, own, other, grads, far):
    def kernel(at_ref, own_ref, other_ref, grads, far_ref, out_ref):
        last = times(grads[...], far_ref[...])
        flipped = at_ref[1] == 1
        missing = lax.rem(at_ref[0] + 2, 4)
        parts = []
        for x in range(4):
            mine = own_ref[:, x * 160 : x * 160 + 160]
            theirs = jnp.where(missing == x, last, other_ref[:, x * 160 : x * 160 + 160])
            parts += [jnp.where(flipped, theirs, mine), jnp.where(flipped, mine, theirs)]
        out_ref[...] = jnp.concatenate(parts, axis=1)

    whole = pl.BlockSpec(memory_space=pltpu.VMEM)
    return pl.pallas_call(
        kernel,
        in_specs=[pl.BlockSpec(memory_space=pltpu.SMEM)] + [whole] * 4,
        out_specs=whole,
        out_shape=jax.ShapeDtypeStruct((256, 1280), jnp.float32),
        compiler_params=pltpu.CompilerParams(vmem_limit_bytes=VMEM),
        cost_estimate=SHORT,
        name="finish",
    )(at, own, other, grads, far)


def local(train_acts, train_cots, train_len, test_grads, proj_in, proj_out):
    x, yh, z, core = (lax.axis_index(name) for name in ("x", "yh", "z", "c"))
    scalars = scalar_table(z, core, train_len)

    acts = train_acts.reshape(8, 2, 2, 512, 128)
    cots = train_cots.reshape(8, 2, 2, 512, 128)

    away = project(1, scalars, acts, cots, proj_in, proj_out, True)
    arrived = [lax.ppermute(a, "c", SWAP) for a in away]
    kept = project(0, scalars, acts, cots, proj_in, proj_out, False)
    sent = [fold(k, a, True, True) for k, a in zip(kept, arrived)]
    moved = [along_z(a, 0, sign) for a, sign in zip(sent, SIGNS)]
    kept = [fold(k, a, False, False) for k, a in zip(kept, arrived)]
    arrived = moved

    down = [(i, (i - 1) % 4) for i in range(4)]
    up = [(i, (i + 1) % 4) for i in range(4)]
    own1, own3 = lax.ppermute(test_grads, "x", down), lax.ppermute(test_grads, "x", up)
    other0 = lax.ppermute(test_grads, "yh", SWAP)

    sent = [fold(k, a, True, True) for k, a in zip(kept, arrived)]
    moved = [along_z(a, 1, sign) for a, sign in zip(sent, SIGNS)]
    kept = [fold(k, a, False, False) for k, a in zip(kept, arrived)]
    sent, kept = fold_pair(kept, moved)
    arrived = along_z(sent, 2, 1)
    own2 = [lax.ppermute(own1[:80], "x", down), lax.ppermute(own3[80:], "x", up)]
    total, coded = fold_both(kept, arrived)
    arrived = lax.ppermute(coded, "yl", SWAP)
    arrived, own2 = lax.optimization_barrier((arrived, own2))
    other1, other3 = lax.ppermute(other0, "x", down), lax.ppermute(other0, "x", up)
    other2 = lax.ppermute(jnp.concatenate(own2, axis=0), "yh", SWAP)
    grads = outer_grads(total, arrived).reshape(16, 4096)

    held = jnp.concatenate([grads, along_z(grads, 2, 1)], axis=0)
    held = [held[:, :2048], held[:, 2048:]]
    for step in (1, 0):
        got = [along_z(h, step, sign) for h, sign in zip(held, SIGNS)]
        held = [jnp.concatenate([h, g], axis=0) for h, g in zip(held, got)]
    pieces = [piece for h in held for piece in (h, lax.ppermute(h, "c", SWAP))]

    at = jnp.stack([x, yh])
    own = [(test_grads, 0, 0), (own1, 1, 0), (own3, 3, 0), (own2[0], 2, 0), (own2[1], 2, 80)]
    other = [(other0, 0, 0), (other1, 1, 0), (other3, 3, 0)]
    own, other, grads = score(scalars, at, pieces, own, other)
    return finish(at, own, other, grads, other2)


def solution(mesh):
    fine = Mesh(mesh.devices.reshape(4, 2, 8, 2, 2), ("x", "yh", "z", "yl", "c"))
    in_specs = (
        P(GRP, None, HID),
        P(GRP, None, HID),
        P(GRP),
        P(HID + GRP, None),
        P(None, HID),
        P(None, HID),
    )
    return jax.shard_map(local, mesh=fine, in_specs=in_specs, out_specs=P(GRP, HID), check_vma=False)
```

```python
import jax
import jax.numpy as jnp
from jax import lax
from jax.experimental import pallas as pl
from jax.experimental.pallas import tpu as pltpu
from jax.sharding import Mesh, PartitionSpec as P

GRP = ("x", "yh")
HID = ("z", "yl", "c")
SWAP = [(0, 1), (1, 0)]
STEPS = (1, -1, 3)
SIGNS = (1, -1)
BLOCK = 8 * 64 + 16
TOP = 14.0
VMEM = 32 * 1024 * 1024
SHORT = pl.CostEstimate(flops=0, bytes_accessed=0, transcendentals=0)


def z_partner(z, step, sign):
    delta = STEPS[step] * sign
    return (z + (delta if z % 2 == 0 else -delta)) % 8


def along_z(array, step, sign):
    return lax.ppermute(array, "z", [(z, z_partner(z, step, sign)) for z in range(8)])


def in_hbm(array):
    return pltpu.with_memory_space_constraint(array, pltpu.HBM)


def owner_table():
    table = []
    for z in range(8):
        rows = []
        for sign in SIGNS:
            row = []
            for path in range(8):
                at = z
                for step in range(3):
                    if (path >> (2 - step)) & 1:
                        at = z_partner(at, step, sign)
                row.append(at)
            rows.append(row)
        table.append(rows)
    return table


def encode(values):
    top = jnp.max(jnp.abs(values), axis=1)
    power = jnp.ceil(jnp.log2(jnp.maximum(top, 1e-30)))
    codes = jnp.round(values * jnp.exp2(TOP - power)[:, None, :])
    tail = jnp.concatenate([power, jnp.zeros((8, 128), jnp.float32)], axis=0)
    whole = jnp.concatenate([codes.reshape(512, 128), tail], axis=0)
    return whole.astype(jnp.int32).astype(jnp.int16)


def decode(block):
    whole = block.astype(jnp.int32).astype(jnp.float32)
    power = whole[512:520]
    return whole[:512].reshape(8, 64, 128) * jnp.exp2(power - TOP)[:, None, :]


def scalar_table(z, core, lens):
    owner = jnp.asarray(owner_table(), jnp.int32).reshape(-1)
    return jnp.concatenate([jnp.stack([z, core]).astype(jnp.int32), owner, lens])


def owner_at(scalars, q, path):
    return scalars[2 + scalars[0] * 16 + q * 8 + path]


def project_kernel(flip, coded, scalars, acts, cots, proj_in, proj_out, *refs):
    outs, (acts_here, cots_here, in_here, out_here, sems, weight_sems) = refs[:2], refs[2:]
    core = scalars[1] ^ flip
    weights = [
        pltpu.make_async_copy(proj_in, in_here, weight_sems.at[0]),
        pltpu.make_async_copy(proj_out, out_here, weight_sems.at[1]),
    ]
    slots = [(q, path) for q in range(2) for path in range(8)]
    copies = []
    for slot, (q, path) in enumerate(slots):
        at = owner_at(scalars, q, path)
        copies.append(
            [
                pltpu.make_async_copy(acts.at[at, core, q], acts_here.at[slot], sems.at[slot, 0]),
                pltpu.make_async_copy(cots.at[at, core, q], cots_here.at[slot], sems.at[slot, 1]),
            ]
        )
    for pair in [weights] + copies:
        for copy in pair:
            copy.start()
    for copy in weights:
        copy.wait()
    zero = jnp.zeros((64, 128), jnp.bfloat16)
    weight = jnp.concatenate(
        [
            jnp.concatenate([out_here[...], zero], axis=1),
            jnp.concatenate([zero, in_here[...]], axis=1),
        ],
        axis=0,
    )
    rows = lax.broadcasted_iota(jnp.int32, (64, 128), 0)
    for slot, (q, path) in enumerate(slots):
        if slot % 8 == 0:
            for pair in copies[slot : slot + 8]:
                for copy in pair:
                    copy.wait()
        terms = lax.dot_general(
            jnp.concatenate([cots_here[slot], acts_here[slot]], axis=1),
            weight,
            (((1,), (1,)), ((), ())),
            preferred_element_type=jnp.float32,
        ).reshape(8, 64, 128)
        first = 130 + (owner_at(scalars, q, path) * 2 + core) * 16 + q * 8
        terms = jnp.stack([jnp.where(rows < scalars[first + e], terms[e], 0.0) for e in range(8)])
        outs[q][path] = encode(terms) if coded else terms


def project(flip, scalars, acts, cots, proj_in, proj_out, coded):
    if coded:
        shape = jax.ShapeDtypeStruct((8, BLOCK, 128), jnp.int16)
    else:
        shape = jax.ShapeDtypeStruct((8, 8, 64, 128), jnp.float32)

    def kernel(*refs):
        project_kernel(flip, coded, *refs)

    return pl.pallas_call(
        kernel,
        in_specs=[pl.BlockSpec(memory_space=pltpu.SMEM)] + [pl.BlockSpec(memory_space=pltpu.HBM)] * 4,
        out_specs=[pl.BlockSpec(memory_space=pltpu.VMEM)] * 2,
        out_shape=[shape] * 2,
        scratch_shapes=[
            pltpu.VMEM((16, 512, 128), jnp.bfloat16),
            pltpu.VMEM((16, 512, 128), jnp.bfloat16),
            pltpu.VMEM((64, 128), jnp.bfloat16),
            pltpu.VMEM((64, 128), jnp.bfloat16),
            pltpu.SemaphoreType.DMA((16, 2)),
            pltpu.SemaphoreType.DMA((2,)),
        ],
        compiler_params=pltpu.CompilerParams(vmem_limit_bytes=VMEM),
        cost_estimate=SHORT,
        name="project",
    )(scalars, *[in_hbm(a) for a in (acts, cots, proj_in, proj_out)])


def fold(kept, arrived, upper, coded):
    count = kept.shape[0] // 2
    first = count if upper else 0

    def kernel(kept_ref, arrived_ref, out_ref):
        total = kept_ref[0] + decode(arrived_ref[0])
        out_ref[0] = encode(total) if coded else total

    message = pl.BlockSpec((1, BLOCK, 128), lambda i: (i, 0, 0))
    plain = pl.BlockSpec((1, 8, 64, 128), lambda i: (i, 0, 0, 0))
    return pl.pallas_call(
        kernel,
        grid=(count,),
        in_specs=[
            pl.BlockSpec((1, 8, 64, 128), lambda i: (i + first, 0, 0, 0)),
            pl.BlockSpec((1, BLOCK, 128), lambda i: (i + first, 0, 0)),
        ],
        out_specs=message if coded else plain,
        out_shape=jax.ShapeDtypeStruct((count, BLOCK, 128), jnp.int16)
        if coded
        else jax.ShapeDtypeStruct((count, 8, 64, 128), jnp.float32),
        compiler_params=pltpu.CompilerParams(vmem_limit_bytes=VMEM),
        cost_estimate=SHORT,
        name="fold",
    )(kept, arrived)


def fold_both(kept, arrived):
    def kernel(*refs):
        for q in range(2):
            total = refs[q][0] + decode(refs[2 + q][0])
            refs[4][q] = total
            refs[5][q] = encode(total)

    return pl.pallas_call(
        kernel,
        out_shape=[
            jax.ShapeDtypeStruct((2, 8, 64, 128), jnp.float32),
            jax.ShapeDtypeStruct((2, BLOCK, 128), jnp.int16),
        ],
        compiler_params=pltpu.CompilerParams(vmem_limit_bytes=VMEM),
        cost_estimate=SHORT,
        name="fold_both",
    )(*kept, *arrived)


def outer_kernel(kept, arrived, out_ref):
    for q in range(2):
        total = kept[q] + decode(arrived[q])
        for e in range(8):
            outer = lax.dot_general(
                total[e, :, :64],
                total[e, :, 64:],
                (((0,), (0,)), ((), ())),
                precision=lax.Precision.HIGHEST,
                preferred_element_type=jnp.float32,
            )
            out_ref[q * 8 + e] = outer.astype(jnp.bfloat16)


def outer_grads(kept, arrived):
    return pl.pallas_call(
        outer_kernel,
        out_shape=jax.ShapeDtypeStruct((16, 64, 64), jnp.bfloat16),
        compiler_params=pltpu.CompilerParams(vmem_limit_bytes=VMEM),
        cost_estimate=SHORT,
        name="outer",
    )(kept, arrived)


def fetch_tests(x, blocks, tests, sems):
    for at in range(4):
        for block, d, first in blocks:

            @pl.when(lax.rem(x + d, 4) == at)
            def _():
                rows = pl.ds(at * 160 + first, block.shape[0])
                pltpu.make_async_copy(block, tests.at[rows, :], sems.at[at]).start()


def wait_tests(at, tests, sems):
    rows = tests.at[pl.ds(at * 160, 160), :]
    pltpu.make_async_copy(rows, rows, sems.at[at]).wait()


def times(grads, tests):
    return lax.dot_general(
        grads, tests, (((1,), (1,)), ((), ())), preferred_element_type=jnp.float32
    )


def score(scalars, at, pieces, own, other):
    blocks = own + other
    places = [(d, first) for _, d, first in blocks]

    def kernel(scalars, at_ref, *refs):
        pieces, blocks, refs = refs[:4], refs[4 : 4 + len(places)], refs[4 + len(places) :]
        own_ref, other_ref, grads, own_tests, other_tests, sems = refs
        blocks = [(block, *place) for block, place in zip(blocks, places)]
        fetch_tests(at_ref[0], blocks[: len(own)], own_tests, sems.at[0])
        copies = [
            pltpu.make_async_copy(block, other_tests.at[pl.ds(n * 160, 160), :], sems.at[1, n])
            for n, (block, _, _) in enumerate(blocks[len(own) :])
        ]
        for copy in copies:
            copy.start()
        for q in range(2):
            for side in range(2):
                for path in range(8):
                    block = (owner_at(scalars, q, path) * 2 + (scalars[1] ^ side)) * 16
                    rows = pl.ds(pl.multiple_of(block, 16), 16)
                    grads[rows, q * 2048 : (q + 1) * 2048] = pieces[2 * q + side][path * 16 : path * 16 + 16, :]
        for first, last, needs in ((0, 256, (0, 1)), (256, 480, (2,)), (480, 640, (3,))):
            for block in needs:
                wait_tests(block, own_tests, sems.at[0])
            own_ref[:, first:last] = times(grads[...], own_tests[first:last, :])
        for copy in copies:
            copy.wait()
        for first, last in ((0, 256), (256, 480)):
            other_ref[:, first:last] = times(grads[...], other_tests[first:last, :])

    whole = pl.BlockSpec(memory_space=pltpu.VMEM)
    scalar = pl.BlockSpec(memory_space=pltpu.SMEM)
    return pl.pallas_call(
        kernel,
        in_specs=[scalar, scalar] + [whole] * 4 + [pl.BlockSpec(memory_space=pltpu.HBM)] * len(blocks),
        out_specs=[whole] * 3,
        out_shape=[
            jax.ShapeDtypeStruct((256, 640), jnp.float32),
            jax.ShapeDtypeStruct((256, 480), jnp.float32),
            jax.ShapeDtypeStruct((256, 4096), jnp.bfloat16),
        ],
        scratch_shapes=[
            pltpu.VMEM((640, 4096), jnp.bfloat16),
            pltpu.VMEM((480, 4096), jnp.bfloat16),
            pltpu.SemaphoreType.DMA((2, 4)),
        ],
        compiler_params=pltpu.CompilerParams(vmem_limit_bytes=VMEM),
        cost_estimate=SHORT,
        name="score",
    )(scalars, at, *pieces, *[in_hbm(block) for block, _, _ in blocks])


def finish(at, own, other, grads, far):
    def kernel(at_ref, own_ref, other_ref, grads, far_ref, out_ref):
        last = times(grads[...], far_ref[...])
        flipped = at_ref[1] == 1
        first, second, fourth = (other_ref[:, n * 160 : n * 160 + 160] for n in range(3))
        parts = []
        for x in range(4):
            mine = own_ref[:, x * 160 : x * 160 + 160]
            d = lax.rem(x + 4 - at_ref[0], 4)
            theirs = jnp.where(d == 0, first, jnp.where(d == 1, second, jnp.where(d == 2, last, fourth)))
            parts += [jnp.where(flipped, theirs, mine), jnp.where(flipped, mine, theirs)]
        out_ref[...] = jnp.concatenate(parts, axis=1)

    whole = pl.BlockSpec(memory_space=pltpu.VMEM)
    return pl.pallas_call(
        kernel,
        in_specs=[pl.BlockSpec(memory_space=pltpu.SMEM)] + [whole] * 4,
        out_specs=whole,
        out_shape=jax.ShapeDtypeStruct((256, 1280), jnp.float32),
        compiler_params=pltpu.CompilerParams(vmem_limit_bytes=VMEM),
        cost_estimate=SHORT,
        name="finish",
    )(at, own, other, grads, far)


def local(train_acts, train_cots, train_len, test_grads, proj_in, proj_out):
    x, yh, z, core = (lax.axis_index(name) for name in ("x", "yh", "z", "c"))
    scalars = scalar_table(z, core, train_len)

    acts = train_acts.reshape(8, 2, 2, 512, 128)
    cots = train_cots.reshape(8, 2, 2, 512, 128)

    away = project(1, scalars, acts, cots, proj_in, proj_out, True)
    arrived = [lax.ppermute(a, "c", SWAP) for a in away]
    kept = project(0, scalars, acts, cots, proj_in, proj_out, False)
    sent = [fold(k, a, True, True) for k, a in zip(kept, arrived)]
    moved = [along_z(a, 0, sign) for a, sign in zip(sent, SIGNS)]
    kept = [fold(k, a, False, False) for k, a in zip(kept, arrived)]
    arrived = moved

    down = [(i, (i - 1) % 4) for i in range(4)]
    up = [(i, (i + 1) % 4) for i in range(4)]
    own1, own3 = lax.ppermute(test_grads, "x", down), lax.ppermute(test_grads, "x", up)
    other0 = lax.ppermute(test_grads, "yh", SWAP)

    for step in (1, 2):
        sent = [fold(k, a, True, True) for k, a in zip(kept, arrived)]
        moved = [along_z(a, step, sign) for a, sign in zip(sent, SIGNS)]
        kept = [fold(k, a, False, False) for k, a in zip(kept, arrived)]
        arrived = moved
    own2 = [lax.ppermute(own1[:80], "x", down), lax.ppermute(own3[80:], "x", up)]
    total, coded = fold_both(kept, arrived)
    arrived = lax.ppermute(coded, "yl", SWAP)
    other2 = lax.ppermute(jnp.concatenate(own2, axis=0), "yh", SWAP)
    arrived, own2 = lax.optimization_barrier((arrived, own2))
    other1, other3 = lax.ppermute(other0, "x", down), lax.ppermute(other0, "x", up)
    grads = outer_grads(total, arrived).reshape(16, 4096)

    held = [grads[:, :2048], grads[:, 2048:]]
    for step in (2, 1, 0):
        got = [along_z(h, step, sign) for h, sign in zip(held, SIGNS)]
        held = [jnp.concatenate([h, g], axis=0) for h, g in zip(held, got)]
    pieces = [piece for h in held for piece in (h, lax.ppermute(h, "c", SWAP))]

    at = jnp.stack([x, yh])
    own = [(test_grads, 0, 0), (own1, 1, 0), (own3, 3, 0), (own2[0], 2, 0), (own2[1], 2, 80)]
    other = [(other0, 0, 0), (other1, 1, 0), (other3, 3, 0)]
    own, other, grads = score(scalars, at, pieces, own, other)
    return finish(at, own, other, grads, other2)


def solution(mesh):
    fine = Mesh(mesh.devices.reshape(4, 2, 8, 2, 2), ("x", "yh", "z", "yl", "c"))
    in_specs = (
        P(GRP, None, HID),
        P(GRP, None, HID),
        P(GRP),
        P(HID + GRP, None),
        P(None, HID),
        P(None, HID),
    )
    return jax.shard_map(local, mesh=fine, in_specs=in_specs, out_specs=P(GRP, HID), check_vma=False)
```

```python
import jax
import jax.numpy as jnp
from jax import lax
from jax.experimental import pallas as pl
from jax.experimental.pallas import tpu as pltpu
from jax.sharding import Mesh, PartitionSpec as P

GRP = ("x", "yh")
HID = ("z", "yl", "c")
SWAP = [(0, 1), (1, 0)]
STEPS = (1, -1, 3)
SIGNS = (1, -1)
BLOCK = 8 * 64 + 16
TOP = 14.0
VMEM = 32 * 1024 * 1024


def z_partner(z, step, sign):
    delta = STEPS[step] * sign
    return (z + (delta if z % 2 == 0 else -delta)) % 8


def along_z(array, step, sign):
    return lax.ppermute(array, "z", [(z, z_partner(z, step, sign)) for z in range(8)])


def in_hbm(array):
    return pltpu.with_memory_space_constraint(array, pltpu.HBM)


def owner_table():
    table = []
    for z in range(8):
        rows = []
        for sign in SIGNS:
            row = []
            for path in range(8):
                at = z
                for step in range(3):
                    if (path >> (2 - step)) & 1:
                        at = z_partner(at, step, sign)
                row.append(at)
            rows.append(row)
        table.append(rows)
    return table


def encode(values):
    top = jnp.max(jnp.abs(values), axis=1)
    power = jnp.ceil(jnp.log2(jnp.maximum(top, 1e-30)))
    codes = jnp.round(values * jnp.exp2(TOP - power)[:, None, :])
    tail = jnp.concatenate([power, jnp.zeros((8, 128), jnp.float32)], axis=0)
    whole = jnp.concatenate([codes.reshape(512, 128), tail], axis=0)
    return whole.astype(jnp.int32).astype(jnp.int16)


def decode(block):
    whole = block.astype(jnp.int32).astype(jnp.float32)
    power = whole[512:520]
    return whole[:512].reshape(8, 64, 128) * jnp.exp2(power - TOP)[:, None, :]


def scalar_table(z, core, lens):
    owner = jnp.asarray(owner_table(), jnp.int32).reshape(-1)
    return jnp.concatenate([jnp.stack([z, core]).astype(jnp.int32), owner, lens])


def owner_at(scalars, q, path):
    return scalars[2 + scalars[0] * 16 + q * 8 + path]


def project_kernel(flip, coded, scalars, acts, cots, proj_in, proj_out, *refs):
    outs, (acts_here, cots_here, in_here, out_here, sems, weight_sems) = refs[:2], refs[2:]
    core = scalars[1] ^ flip
    weights = [
        pltpu.make_async_copy(proj_in, in_here, weight_sems.at[0]),
        pltpu.make_async_copy(proj_out, out_here, weight_sems.at[1]),
    ]
    slots = [(q, path) for q in range(2) for path in range(8)]
    copies = []
    for slot, (q, path) in enumerate(slots):
        at = owner_at(scalars, q, path)
        copies.append(
            [
                pltpu.make_async_copy(acts.at[at, core, q], acts_here.at[slot], sems.at[slot, 0]),
                pltpu.make_async_copy(cots.at[at, core, q], cots_here.at[slot], sems.at[slot, 1]),
            ]
        )
    for pair in [weights] + copies:
        for copy in pair:
            copy.start()
    for copy in weights:
        copy.wait()
    zero = jnp.zeros((64, 128), jnp.bfloat16)
    weight = jnp.concatenate(
        [
            jnp.concatenate([out_here[...], zero], axis=1),
            jnp.concatenate([zero, in_here[...]], axis=1),
        ],
        axis=0,
    )
    rows = lax.broadcasted_iota(jnp.int32, (64, 128), 0)
    for slot, (q, path) in enumerate(slots):
        if slot % 8 == 0:
            for pair in copies[slot : slot + 8]:
                for copy in pair:
                    copy.wait()
        terms = lax.dot_general(
            jnp.concatenate([cots_here[slot], acts_here[slot]], axis=1),
            weight,
            (((1,), (1,)), ((), ())),
            preferred_element_type=jnp.float32,
        ).reshape(8, 64, 128)
        first = 130 + (owner_at(scalars, q, path) * 2 + core) * 16 + q * 8
        terms = jnp.stack([jnp.where(rows < scalars[first + e], terms[e], 0.0) for e in range(8)])
        outs[q][path] = encode(terms) if coded else terms


def project(flip, scalars, acts, cots, proj_in, proj_out, coded):
    if coded:
        shape = jax.ShapeDtypeStruct((8, BLOCK, 128), jnp.int16)
    else:
        shape = jax.ShapeDtypeStruct((8, 8, 64, 128), jnp.float32)

    def kernel(*refs):
        project_kernel(flip, coded, *refs)

    return pl.pallas_call(
        kernel,
        in_specs=[pl.BlockSpec(memory_space=pltpu.SMEM)] + [pl.BlockSpec(memory_space=pltpu.HBM)] * 4,
        out_specs=[pl.BlockSpec(memory_space=pltpu.VMEM)] * 2,
        out_shape=[shape] * 2,
        scratch_shapes=[
            pltpu.VMEM((16, 512, 128), jnp.bfloat16),
            pltpu.VMEM((16, 512, 128), jnp.bfloat16),
            pltpu.VMEM((64, 128), jnp.bfloat16),
            pltpu.VMEM((64, 128), jnp.bfloat16),
            pltpu.SemaphoreType.DMA((16, 2)),
            pltpu.SemaphoreType.DMA((2,)),
        ],
        compiler_params=pltpu.CompilerParams(vmem_limit_bytes=VMEM),
        name="project",
    )(scalars, *[in_hbm(a) for a in (acts, cots, proj_in, proj_out)])


def fold(kept, arrived, upper, coded):
    count = kept.shape[0] // 2
    first = count if upper else 0

    def kernel(kept_ref, arrived_ref, out_ref):
        total = kept_ref[0] + decode(arrived_ref[0])
        out_ref[0] = encode(total) if coded else total

    message = pl.BlockSpec((1, BLOCK, 128), lambda i: (i, 0, 0))
    plain = pl.BlockSpec((1, 8, 64, 128), lambda i: (i, 0, 0, 0))
    return pl.pallas_call(
        kernel,
        grid=(count,),
        in_specs=[
            pl.BlockSpec((1, 8, 64, 128), lambda i: (i + first, 0, 0, 0)),
            pl.BlockSpec((1, BLOCK, 128), lambda i: (i + first, 0, 0)),
        ],
        out_specs=message if coded else plain,
        out_shape=jax.ShapeDtypeStruct((count, BLOCK, 128), jnp.int16)
        if coded
        else jax.ShapeDtypeStruct((count, 8, 64, 128), jnp.float32),
        compiler_params=pltpu.CompilerParams(vmem_limit_bytes=VMEM),
        name="fold",
    )(kept, arrived)


def fold_both(kept, arrived):
    def kernel(kept_ref, arrived_ref, total_ref, coded_ref):
        total = kept_ref[0] + decode(arrived_ref[0])
        total_ref[0] = total
        coded_ref[0] = encode(total)

    return pl.pallas_call(
        kernel,
        out_shape=[
            jax.ShapeDtypeStruct((1, 8, 64, 128), jnp.float32),
            jax.ShapeDtypeStruct((1, BLOCK, 128), jnp.int16),
        ],
        compiler_params=pltpu.CompilerParams(vmem_limit_bytes=VMEM),
        name="fold_both",
    )(kept, arrived)


def outer_kernel(kept0, kept1, arrived0, arrived1, out_ref):
    for q, (kept, arrived) in enumerate(((kept0, arrived0), (kept1, arrived1))):
        total = kept[0] + decode(arrived[0])
        for e in range(8):
            outer = lax.dot_general(
                total[e, :, :64],
                total[e, :, 64:],
                (((0,), (0,)), ((), ())),
                precision=lax.Precision.HIGHEST,
                preferred_element_type=jnp.float32,
            )
            out_ref[q * 8 + e] = outer.astype(jnp.bfloat16)


def outer_grads(kept, arrived):
    return pl.pallas_call(
        outer_kernel,
        out_shape=jax.ShapeDtypeStruct((16, 64, 64), jnp.bfloat16),
        compiler_params=pltpu.CompilerParams(vmem_limit_bytes=VMEM),
        name="outer",
    )(*kept, *arrived)


def load_tests(x, blocks, tests, sems):
    for at in range(4):
        for block, d, first in blocks:

            @pl.when(lax.rem(x + d, 4) == at)
            def _():
                rows = pl.ds(at * 160 + first, block.shape[0])
                pltpu.make_async_copy(block, tests.at[rows, :], sems.at[at]).start()


def wait_tests(at, tests, sems):
    rows = tests.at[pl.ds(at * 160, 160), :]
    pltpu.make_async_copy(rows, rows, sems.at[at]).wait()


def place_grads(scalars, pieces, grads):
    for q in range(2):
        for side in range(2):
            for path in range(8):
                at = (owner_at(scalars, q, path) * 2 + (scalars[1] ^ side)) * 16
                rows = pl.ds(pl.multiple_of(at, 16), 16)
                grads[rows, q * 2048 : (q + 1) * 2048] = pieces[2 * q + side][path * 16 : path * 16 + 16, :]


def multiply(grads, tests, sems, out):
    for first, last, needs in ((0, 256, (0, 1)), (256, 480, (2,)), (480, 640, (3,))):
        for at in needs:
            wait_tests(at, tests, sems)
        out[:, first:last] = lax.dot_general(
            grads[...],
            tests[first:last, :],
            (((1,), (1,)), ((), ())),
            preferred_element_type=jnp.float32,
        )


def score_kernel(places, scalars, at_ref, *refs):
    pieces, blocks, refs = refs[:4], refs[4 : 4 + len(places)], refs[4 + len(places) :]
    out_ref, grads, tests, sems = refs
    load_tests(at_ref[0], [(b, *p) for b, p in zip(blocks, places)], tests, sems)
    place_grads(scalars, pieces, grads)
    multiply(grads, tests, sems, out_ref)


def finish_kernel(places, scalars, at_ref, *refs):
    pieces, blocks, refs = refs[:4], refs[4 : 4 + len(places)], refs[4 + len(places) :]
    own_ref, out_ref, grads, tests, sems, part = refs
    load_tests(at_ref[0], [(b, *p) for b, p in zip(blocks, places)], tests, sems)
    place_grads(scalars, pieces, grads)
    multiply(grads, tests, sems, part)
    flipped = at_ref[1] == 1
    own, other = own_ref[...], part[...]
    low, high = jnp.where(flipped, other, own), jnp.where(flipped, own, other)
    parts = []
    for x in range(4):
        parts += [low[:, x * 160 : x * 160 + 160], high[:, x * 160 : x * 160 + 160]]
    out_ref[...] = jnp.concatenate(parts, axis=1)


def score(scalars, at, pieces, blocks, own=None):
    places = [(d, first) for _, d, first in blocks]
    body = score_kernel if own is None else finish_kernel

    def kernel(*refs):
        body(places, *refs)

    whole = pl.BlockSpec(memory_space=pltpu.VMEM)
    scalar = pl.BlockSpec(memory_space=pltpu.SMEM)
    extra = [] if own is None else [own]
    scratch = [
        pltpu.VMEM((256, 4096), jnp.bfloat16),
        pltpu.VMEM((640, 4096), jnp.bfloat16),
        pltpu.SemaphoreType.DMA((4,)),
    ]
    if own is not None:
        scratch.append(pltpu.VMEM((256, 640), jnp.float32))
    return pl.pallas_call(
        kernel,
        in_specs=[scalar, scalar]
        + [whole] * 4
        + [pl.BlockSpec(memory_space=pltpu.HBM)] * len(blocks)
        + [whole] * len(extra),
        out_specs=whole,
        out_shape=jax.ShapeDtypeStruct((256, 640 if own is None else 1280), jnp.float32),
        scratch_shapes=scratch,
        compiler_params=pltpu.CompilerParams(vmem_limit_bytes=VMEM),
        name="score" if own is None else "finish",
    )(scalars, at, *pieces, *[in_hbm(block) for block, _, _ in blocks], *extra)


def local(train_acts, train_cots, train_len, test_grads, proj_in, proj_out):
    x, yh, z, core = (lax.axis_index(name) for name in ("x", "yh", "z", "c"))
    scalars = scalar_table(z, core, train_len)

    acts = train_acts.reshape(8, 2, 2, 512, 128)
    cots = train_cots.reshape(8, 2, 2, 512, 128)

    down = [(i, (i - 1) % 4) for i in range(4)]
    up = [(i, (i + 1) % 4) for i in range(4)]
    own1, own3 = lax.ppermute(test_grads, "x", down), lax.ppermute(test_grads, "x", up)
    other0 = lax.ppermute(test_grads, "yh", SWAP)

    away = project(1, scalars, acts, cots, proj_in, proj_out, True)
    arrived = [lax.ppermute(a, "c", SWAP) for a in away]
    kept = project(0, scalars, acts, cots, proj_in, proj_out, False)
    sent = [fold(k, a, True, True) for k, a in zip(kept, arrived)]
    moved = [along_z(a, 0, sign) for a, sign in zip(sent, SIGNS)]
    kept = [fold(k, a, False, False) for k, a in zip(kept, arrived)]
    arrived = moved

    for step in (1, 2):
        sent = [fold(k, a, True, True) for k, a in zip(kept, arrived)]
        moved = [along_z(a, step, sign) for a, sign in zip(sent, SIGNS)]
        kept = [fold(k, a, False, False) for k, a in zip(kept, arrived)]
        arrived = moved
        if step == 1:
            arrived, own1, own3, other0 = lax.optimization_barrier((arrived, own1, own3, other0))
            own2 = [lax.ppermute(own1[:80], "x", down), lax.ppermute(own3[80:], "x", up)]
    both = [fold_both(k, a) for k, a in zip(kept, arrived)]
    arrived = [lax.ppermute(coded, "yl", SWAP) for _, coded in both]
    arrived, own2 = lax.optimization_barrier((arrived, own2))
    other1, other3 = lax.ppermute(other0, "x", down), lax.ppermute(other0, "x", up)
    other2 = lax.ppermute(jnp.concatenate(own2, axis=0), "yh", SWAP)
    grads = outer_grads([total for total, _ in both], arrived).reshape(16, 4096)

    held = [grads[:, :2048], grads[:, 2048:]]
    for step in (2, 1, 0):
        got = [along_z(h, step, sign) for h, sign in zip(held, SIGNS)]
        held = [jnp.concatenate([h, g], axis=0) for h, g in zip(held, got)]
    pieces = [piece for h in held for piece in (h, lax.ppermute(h, "c", SWAP))]

    at = jnp.stack([x, yh])
    blocks = [(test_grads, 0, 0), (own1, 1, 0), (own3, 3, 0), (own2[0], 2, 0), (own2[1], 2, 80)]
    own = score(scalars, at, pieces, blocks)
    blocks = [(other0, 0, 0), (other1, 1, 0), (other2, 2, 0), (other3, 3, 0)]
    return score(scalars, at, pieces, blocks, own)


def solution(mesh):
    fine = Mesh(mesh.devices.reshape(4, 2, 8, 2, 2), ("x", "yh", "z", "yl", "c"))
    in_specs = (
        P(GRP, None, HID),
        P(GRP, None, HID),
        P(GRP),
        P(HID + GRP, None),
        P(None, HID),
        P(None, HID),
    )
    return jax.shard_map(local, mesh=fine, in_specs=in_specs, out_specs=P(GRP, HID), check_vma=False)
```
